32 devices in a mesh: rep: 16 (over z, y, x), tp: 2 (over core).
Axes of the slice: x: 2, y: 2, z: 4, core: 2. Of those that a mesh axis runs over, the one named last changes fastest.
Arguments:
- hidden_input: bfloat16 [16384, 8192], P('rep', 'tp'), may hold values from -6 to 6
- query_weight: bfloat16 [8192, 4096], P('tp'), may hold values from -0.0625 to 0.0625
- slot_down_weight: bfloat16 [64, 8192, 64], P('rep', 'tp'), may hold values from -0.0625 to 0.0625
- slot_up_weight: bfloat16 [64, 64, 4096], P('rep', None, 'tp'), may hold values from -0.75 to 0.75
- request_adapter: int32 [16384, 1], P('rep'), may hold values from 0 to 63; in each aligned block of 1024 rows (0 to 1023, 1024 to 2047, ...) at most 16 rows name the same one
- adapter_slot: int32 [64], replicated, may hold values from 0 to 63, each once
Outputs:
- queries: bfloat16 [16384, 4096], P('rep', 'tp')
The draws below stay inside these ranges and needn't reach their ends.
Inputs may be any that keep to these rules, and one draw needn't show every extreme that they name: `request_adapter`: within the requests of one index of rep no adapter is named more than 16 times. `adapter_slot`: each slot once; slot s is stored by index s // 4 of rep, at position s % 4.
All inputs are finite; a program needn't handle non-finite values.
Results may differ from the reference program's by a relative error of at most 0.012.
Values may be sent and summed in bfloat16 or wider, within the bound.
No kernel may reach another device: no remote copies, remote signals or barrier semaphores. Data moves between devices by JAX's collectives and lax.ppermute only.
A program may use at most 256 MiB of HBM per device.

```python
import math
import jax
import jax.numpy as jnp
import numpy as np
from jax import lax

MODEL_WIDTH = 8192
QUERY_WIDTH = 4096
ADAPTER_RANK = 64
MOST = 16
ROWS_DEV = 1024
ADAPTER_COUNT = 64
TOKENS = 16384
N_TP = 2


def level_of(stream_key, dims, pieces, least, high):
    gain, own = 1.0, jax.random.fold_in(stream_key, 6)
    for dim, parts in pieces:
        heights = jnp.exp(jax.random.uniform(jax.random.fold_in(own, dim), (parts,), jnp.float32, least / len(pieces), high / len(pieces)))
        gain = gain * jnp.repeat(heights, dims[dim] // parts).reshape([-1 if axis == dim else 1 for axis in range(len(dims))])
    return gain


def routed_block(rng, own, number, rows, amount, top, bound, skew):
    order = jax.random.permutation(rng, amount)
    crowded, common = shares(amount, rows * top, bound, skew, True), shares(amount, rows * top, bound, skew, False)
    places = jnp.arange(amount)

    def named(tallies, turn):
        used = int((tallies > 0).sum())
        fixed = max(1, used // 4)
        passed = fixed + (places - fixed + turn * (used - fixed)) % max(1, amount - fixed)
        return jnp.zeros((amount,), jnp.int32).at[order[jnp.where(places < fixed, places, passed)]].set(jnp.asarray(tallies, jnp.int32))

    tallies = jnp.where(number % 4 == 0, named(crowded, number // 4), named(common, number - number // 4 - 1))
    mixed = jax.random.permutation(jax.random.fold_in(own, 3), amount)
    source_of, receiver = mixed[0:amount // 2 * 2:2], mixed[1:amount // 2 * 2:2]
    margin = jnp.minimum(tallies[source_of] - 1, bound - tallies[receiver]) // 2
    margin = jnp.where((source_of == order[0]) | (receiver == order[0]) | (tallies[receiver] == 0), 0, jnp.maximum(margin, 0))
    passed = jax.random.randint(jax.random.fold_in(own, 4), (amount // 2,), 0, 1 << 20) % (margin + 1)
    tallies = tallies.at[source_of].add(-passed).at[receiver].add(passed)
    members = jnp.searchsorted(jnp.cumsum(tallies), jnp.arange(rows * top), side="right").astype(jnp.int32)
    grid = members.reshape(top, rows).T
    grid = grid[jax.random.permutation(jax.random.fold_in(own, 1), rows)]
    turn = jax.random.randint(jax.random.fold_in(own, 2), (rows, 1), 0, top)
    return jnp.take_along_axis(grid, (jnp.arange(top)[None, :] + turn) % top, axis=1)


def shares(count, total, reach, lean, full):
    portions = [(1 << 20) // math.isqrt(grade ** lean) + 1 for grade in range(1, count + 1)]
    largest = reach if full else min(reach, max(-(-total // count), total * portions[0] // sum(portions)))
    least = 1 if total - largest >= count - 1 else 0
    given, spare = [largest] + [least] * (count - 1), total - largest - least * (count - 1)
    while spare > 0:
        free = [i for i in range(1, count) if given[i] < largest] or [i for i in range(1, count) if given[i] < reach]
        whole, remaining = sum([portions[i] for i in free]), spare
        for i in free:
            extra = min(reach - given[i], max(1, remaining * portions[i] // whole), spare)
            given[i] = given[i] + extra
            spare = spare - extra
    return np.array(given)


def noise(rng, dims, deviation, reach, cuts=(), kind=jnp.bfloat16):
    drawn = deviation * jax.random.normal(rng, dims, jnp.float32)
    if cuts:
        drawn = drawn * level_of(rng, dims, cuts, -0.22, 0.18)
    return jnp.clip(drawn, -reach, reach).astype(kind)


def setup_inputs(seed: int = 0) -> dict:
    keys = jax.random.split(jax.random.key(seed), 7)
    hidden_input = noise(keys[0], (TOKENS, MODEL_WIDTH), 1.0, 6.0, ((0, 16), (1, 2)))
    query_weight = noise(keys[1], (MODEL_WIDTH, QUERY_WIDTH), MODEL_WIDTH ** -0.5, 0.0625, ((0, 2),))
    slot_down_weight = noise(keys[2], (ADAPTER_COUNT, MODEL_WIDTH, ADAPTER_RANK), MODEL_WIDTH ** -0.5, 0.0625, ((0, 16), (1, 2)))
    slot_up_weight = noise(keys[3], (ADAPTER_COUNT, ADAPTER_RANK, QUERY_WIDTH), ADAPTER_RANK ** -0.5, 0.75, ((0, 16), (2, 2)))
    request_adapter_keys = jax.random.split(jax.random.fold_in(keys[4], 1), TOKENS // ROWS_DEV)
    request_adapter_turns = jax.random.permutation(jax.random.fold_in(keys[4], 3), TOKENS // ROWS_DEV)
    request_adapter = jax.vmap(lambda own, number: routed_block(jax.random.fold_in(keys[4], 2), own, number, ROWS_DEV, ADAPTER_COUNT, 1, MOST, 2))(request_adapter_keys, request_adapter_turns).reshape((TOKENS, 1))
    adapter_slot = jax.random.permutation(keys[5], ADAPTER_COUNT).astype(jnp.int32)
    return {"hidden_input": hidden_input, "query_weight": query_weight, "slot_down_weight": slot_down_weight, "slot_up_weight": slot_up_weight, "request_adapter": request_adapter, "adapter_slot": adapter_slot}


def reference(hidden_input, query_weight, slot_down_weight, slot_up_weight, request_adapter, adapter_slot):
    width = MODEL_WIDTH // N_TP
    base = jnp.zeros((TOKENS, QUERY_WIDTH), jnp.float32)
    for block in range(N_TP):
        part = jnp.dot(hidden_input[:, block * width:(block + 1) * width], query_weight[block * width:(block + 1) * width, :], preferred_element_type=jnp.float32).astype(jnp.bfloat16)
        part = lax.optimization_barrier(part)
        base = base + part.astype(jnp.float32)
    slots = adapter_slot[request_adapter[:, 0]].astype(jnp.int32)
    step_rows = 32
    blocks = TOKENS // step_rows

    def one_block(index):
        start = (index * step_rows).astype(jnp.int32)
        rows = lax.dynamic_slice_in_dim(hidden_input, start, step_rows, 0).astype(jnp.float32)
        picked_adapter = lax.dynamic_slice_in_dim(slots, start, step_rows, 0)
        down_matrices = slot_down_weight[picked_adapter].astype(jnp.float32)
        low = jnp.einsum("id,idr->ir", rows, down_matrices).astype(jnp.bfloat16)
        up_matrices = slot_up_weight[picked_adapter].astype(jnp.float32)
        return jnp.einsum("ir,irq->iq", low.astype(jnp.float32), up_matrices).astype(jnp.bfloat16)

    lift = lax.map(one_block, jnp.arange(blocks, dtype=jnp.int32)).reshape(TOKENS, QUERY_WIDTH)
    return (base + lift.astype(jnp.float32)).astype(jnp.bfloat16)
```

```python
import functools

import jax
import jax.numpy as jnp
from jax import lax
from jax.experimental import pallas as pl
from jax.experimental.pallas import tpu as pltpu
from jax.sharding import PartitionSpec as P

MOST = 16
COLUMNS = 4
PLANES = 4
SWAP = [(0, 1), (1, 0)]
LIMIT = 56 * 1024 * 1024
NT = (((1,), (1,)), ((), ()))


def params(steps=1):
    return pltpu.CompilerParams(dimension_semantics=("arbitrary",) * steps, vmem_limit_bytes=LIMIT)


def cost(flops, size):
    return pl.CostEstimate(flops=flops, bytes_accessed=size, transcendentals=0)


def pack_kernel(target_ref, x_ref, *rest):
    outs, onehot = rest[:-1], rest[-1]
    size = onehot.shape[0]

    @pl.when(pl.program_id(0) == 0)
    def _():
        place = lax.broadcasted_iota(jnp.int32, onehot.shape, 0)
        onehot[...] = (place == target_ref[...]).astype(jnp.bfloat16)

    packed = jnp.dot(onehot[...], x_ref[...], preferred_element_type=jnp.float32).astype(jnp.bfloat16)
    part = size // len(outs)
    for k, out in enumerate(outs):
        out[...] = packed[k * part : (k + 1) * part]


def pack(target, x, parts):
    rows, width = x.shape
    tile = 512
    part = rows // parts
    return pl.pallas_call(
        pack_kernel,
        grid=(width // tile,),
        in_specs=[pl.BlockSpec((1, rows), lambda i: (0, 0)), pl.BlockSpec((rows, tile), lambda i: (0, i))],
        out_specs=[pl.BlockSpec((part, tile), lambda i: (0, i))] * parts,
        out_shape=[jax.ShapeDtypeStruct((part, width), x.dtype)] * parts,
        scratch_shapes=[pltpu.VMEM((rows, rows), jnp.bfloat16)],
        compiler_params=params(),
        cost_estimate=cost(2 * rows * rows * width, 4 * rows * width),
        name="pack_rows",
    )(target, x)


def project_kernel(place_ref, x_ref, w_ref, o_ref):
    o_ref[...] = jnp.dot(x_ref[...], w_ref[...], preferred_element_type=jnp.float32).astype(o_ref.dtype)


def project(half, x, w):
    rows, width = x.shape
    columns = w.shape[1] // 2
    tile = 256
    steps = columns // tile
    return pl.pallas_call(
        project_kernel,
        grid_spec=pltpu.PrefetchScalarGridSpec(
            num_scalar_prefetch=1,
            grid=(steps,),
            in_specs=[
                pl.BlockSpec((rows, width), lambda i, place: (0, 0)),
                pl.BlockSpec((width, tile), lambda i, place: (0, place[0] * steps + i)),
            ],
            out_specs=pl.BlockSpec((rows, tile), lambda i, place: (0, i)),
        ),
        out_shape=jax.ShapeDtypeStruct((rows, columns), jnp.bfloat16),
        compiler_params=params(),
        cost_estimate=cost(2 * rows * width * columns, 2 * (rows * width + columns * width + rows * columns)),
        name="project_half",
    )(half.reshape(1), x, w)


def down_kernel(*refs):
    xs, w_ref, o_ref = refs[:-2], refs[-2], refs[-1]
    rows = jnp.concatenate([x[...] for x in xs], axis=0)
    o_ref[...] = lax.dot_general(rows, w_ref[...], NT, preferred_element_type=jnp.float32)


def down(xs, w, start):
    adapters, rank, width = w.shape
    return pl.pallas_call(
        down_kernel,
        grid=(adapters,),
        in_specs=[pl.BlockSpec((MOST, width), lambda i: (start + i, 0))] * len(xs)
        + [pl.BlockSpec((None, rank, width), lambda i: (i, 0, 0))],
        out_specs=pl.BlockSpec((None, len(xs) * MOST, rank), lambda i: (i, 0, 0)),
        out_shape=jax.ShapeDtypeStruct((adapters, len(xs) * MOST, rank), jnp.float32),
        compiler_params=params(),
        cost_estimate=cost(
            2 * adapters * len(xs) * MOST * rank * width, 2 * adapters * width * (rank + len(xs) * MOST)
        ),
        name="down_rows",
    )(*xs, w)


def lift_kernel(y_ref, u_ref, *outs):
    rows = jnp.dot(y_ref[...], u_ref[...], preferred_element_type=jnp.float32).astype(jnp.bfloat16)
    for k, out in enumerate(outs):
        out[...] = rows[k * MOST : (k + 1) * MOST]


def lift(y, u):
    adapters, rank, columns = u.shape
    rows = y.shape[1]
    parts = rows // MOST
    return pl.pallas_call(
        lift_kernel,
        grid=(adapters,),
        in_specs=[
            pl.BlockSpec((None, rows, rank), lambda i: (i, 0, 0)),
            pl.BlockSpec((None, rank, columns), lambda i: (i, 0, 0)),
        ],
        out_specs=[pl.BlockSpec((MOST, columns), lambda i: (i, 0))] * parts,
        out_shape=[jax.ShapeDtypeStruct((adapters * MOST, columns), jnp.bfloat16)] * parts,
        compiler_params=params(),
        cost_estimate=cost(2 * adapters * rows * rank * columns, 2 * adapters * columns * (rank + rows)),
        name="lift_rows",
    )(y, u)


def finish_kernel(target_ref, own_ref, other_ref, *rest):
    pieces, o_ref, onehot = rest[:-2], rest[-2], rest[-1]

    @pl.when(pl.program_id(0) == 0)
    def _():
        place = lax.broadcasted_iota(jnp.int32, onehot.shape, 1)
        onehot[...] = (place == target_ref[...]).astype(jnp.bfloat16)

    lifted = jnp.concatenate([piece[...] for piece in pieces], axis=0)
    total = jnp.dot(onehot[...], lifted, preferred_element_type=jnp.float32)
    base = own_ref[...].astype(jnp.float32) + other_ref[...].astype(jnp.float32)
    o_ref[...] = (base + total).astype(o_ref.dtype)


def finish(target, own, other, pieces):
    rows, columns = own.shape
    tile = 512
    places = sum(piece.shape[0] for piece in pieces)
    return pl.pallas_call(
        finish_kernel,
        grid=(columns // tile,),
        in_specs=[pl.BlockSpec((rows, 1), lambda i: (0, 0))]
        + [pl.BlockSpec((rows, tile), lambda i: (0, i))] * 2
        + [pl.BlockSpec((piece.shape[0], tile), lambda i: (0, i)) for piece in pieces],
        out_specs=pl.BlockSpec((rows, tile), lambda i: (0, i)),
        out_shape=jax.ShapeDtypeStruct((rows, columns), jnp.bfloat16),
        scratch_shapes=[pltpu.VMEM((rows, places), jnp.bfloat16)],
        compiler_params=params(),
        cost_estimate=cost(2 * rows * places * columns, 8 * rows * columns),
        name="finish_rows",
    )(target, own, other, *pieces)


def places(request_adapter, adapter_slot, total):
    rows = request_adapter.shape[0]
    ids = request_adapter[:, 0]
    names = lax.broadcasted_iota(jnp.int32, (rows, total), 1)
    slots = jnp.sum(jnp.where(ids[:, None] == names, adapter_slot[None, :], 0), axis=1)
    onehot = (slots[:, None] == names).astype(jnp.bfloat16)
    row_iota = lax.broadcasted_iota(jnp.int32, (rows, rows), 0)
    col_iota = lax.broadcasted_iota(jnp.int32, (rows, rows), 1)
    earlier = (row_iota > col_iota).astype(jnp.bfloat16)
    counts = jnp.dot(earlier, onehot, preferred_element_type=jnp.float32)
    position = jnp.sum(counts * onehot.astype(jnp.float32), axis=1).astype(jnp.int32)
    return slots, position


def by_planes(hidden_input, query_weight, slot_down_weight, slot_up_weight, request_adapter, adapter_slot):
    owned = slot_down_weight.shape[0]
    group = owned * MOST
    me = lax.axis_index("rep")
    plane, column = me // COLUMNS, me % COLUMNS
    inner = (plane == 1) | (plane == 2)
    every = range(COLUMNS * PLANES)
    inside = [r for r in every if r // COLUMNS in (1, 2)]
    outside = [r for r in every if r // COLUMNS in (0, 3)]

    def send(x, pairs):
        return lax.ppermute(x, "rep", pairs)

    pair = [(r, r ^ 4) for r in every]
    across = [(r, r ^ 12) for r in inside]
    outward = [(r, r ^ 4) for r in inside]
    turn = [[(r, r ^ d) for r in every] for d in range(COLUMNS)]
    turn_inside = [[(r, r ^ d) for r in inside] for d in range(COLUMNS)]
    turn_inward = [[(r, r ^ 4 ^ d) for r in outside] for d in range(COLUMNS)]

    down_own = jnp.swapaxes(slot_down_weight, 1, 2)
    up_own = slot_up_weight
    down_pair = send(down_own, pair)
    down_near = send(down_own, across)

    slots, position = places(request_adapter, adapter_slot, owned * COLUMNS * PLANES)
    slot_plane = slots // (owned * COLUMNS)
    slot_column = slots // owned % COLUMNS
    far = slot_plane // 2 != plane // 2
    second = jnp.where(far, (slot_plane == 0) | (slot_plane == 3), slot_plane != plane).astype(jnp.int32)
    order = (far.astype(jnp.int32) * COLUMNS + (slot_column ^ column)) * 2 + second
    target = order * group + slots % owned * MOST + position

    packed = pack(target[None, :], hidden_input, 2 * COLUMNS)
    home, away = packed[:COLUMNS], packed[COLUMNS:]
    inward = [send(away[d], turn_inward[d]) for d in range(COLUMNS)]
    beside = [away[0]] + [send(away[d], turn_inside[d]) for d in range(1, COLUMNS)]
    local = [home[0]] + [send(home[d], turn[d]) for d in range(1, COLUMNS)]
    down_far = send(down_pair, across)

    up_pair = send(up_own, pair)
    up_near = send(up_own, across)
    up_far = send(up_pair, across)
    up_near_out = send(up_near, outward)
    up_far_out = send(up_far, outward)
    up_near = jnp.where(inner, up_near, up_near_out)
    up_far = jnp.where(inner, up_far, up_far_out)

    tp = lax.axis_index("tp")
    given = project(1 - tp, hidden_input, query_weight)
    base_other = lax.ppermute(given, "tp", SWAP)
    base_own = project(tp, hidden_input, query_weight)

    def both(y):
        return (y + lax.ppermute(y, "tp", SWAP)).astype(jnp.bfloat16)

    half = COLUMNS * MOST
    lowered = [both(down(local, down_own, 0)), both(down(local, down_pair, owned))]
    for weight, start in ((down_near, 0), (down_far, owned)):
        y = both(down(beside + inward, weight, start))
        lowered.append(jnp.where(inner, y[:, :half], send(y[:, half:], outward)))
    lifted = []
    for y, u in zip(lowered, (up_own, up_pair, up_near, up_far)):
        rows = lift(y, u)
        lifted.append([rows[0]] + [send(rows[d], turn[d]) for d in range(1, COLUMNS)])
    pieces = [lifted[2 * f + s][d] for f in range(2) for d in range(COLUMNS) for s in range(2)]
    return finish(target[:, None], base_own, base_other, pieces)


def by_gather(hidden_input, query_weight, slot_down_weight, slot_up_weight, request_adapter, adapter_slot):
    local_width = hidden_input.shape[1]
    output_width = slot_up_weight.shape[2]
    total = slot_down_weight.shape[0] * lax.axis_size("rep")
    base_sum = lax.psum_scatter(
        lax.dot_general(
            query_weight, hidden_input, (((0,), (1,)), ((), ())), preferred_element_type=jnp.float32
        ).astype(jnp.bfloat16),
        "tp",
        scatter_dimension=0,
        tiled=True,
    ).astype(jnp.float32)
    slots, position = places(request_adapter, adapter_slot, total)
    target = slots * MOST + position
    buffer = jnp.zeros((total * MOST, local_width), jnp.bfloat16).at[target].set(hidden_input)
    slot_rows = buffer.reshape(total, MOST, local_width)
    lowered = jnp.einsum(
        "amd,adr->amr",
        slot_rows,
        lax.all_gather(slot_down_weight, "rep", axis=0, tiled=True),
        preferred_element_type=jnp.float32,
    )
    lowered = lax.psum(lowered.astype(jnp.bfloat16), "tp")
    lifted = jnp.einsum(
        "amr,are->ame",
        lowered,
        lax.all_gather(slot_up_weight, "rep", axis=0, tiled=True),
        preferred_element_type=jnp.float32,
    )
    lift_rows = lifted.astype(jnp.bfloat16).reshape(total * MOST, output_width)[target]
    return (base_sum.T + lift_rows.astype(jnp.float32)).astype(jnp.bfloat16)


def solution(mesh):
    in_specs = (
        P("rep", "tp"),
        P("tp", None),
        P("rep", "tp", None),
        P("rep", None, "tp"),
        P("rep", None),
        P(),
    )
    out_specs = P("rep", "tp")
    planes = mesh.shape["rep"] == COLUMNS * PLANES and mesh.shape["tp"] == 2
    shards = by_planes if planes else by_gather
    return jax.shard_map(shards, mesh=mesh, in_specs=in_specs, out_specs=out_specs, check_vma=False)
```

```python
import functools

import jax
import jax.numpy as jnp
from jax import lax
from jax.experimental import pallas as pl
from jax.experimental.pallas import tpu as pltpu
from jax.sharding import PartitionSpec as P

MOST = 16
COLUMNS = 4
PLANES = 4
SWAP = [(0, 1), (1, 0)]
LIMIT = 56 * 1024 * 1024
NT = (((1,), (1,)), ((), ()))


def params(steps=1):
    return pltpu.CompilerParams(dimension_semantics=("arbitrary",) * steps, vmem_limit_bytes=LIMIT)


def cost(flops, size):
    return pl.CostEstimate(flops=flops, bytes_accessed=size, transcendentals=0)


def pack_kernel(first, target_ref, x_ref, *rest):
    outs, onehot = rest[:-1], rest[-1]

    @pl.when(pl.program_id(0) == 0)
    def _():
        place = lax.broadcasted_iota(jnp.int32, onehot.shape, 0) + first
        onehot[...] = (place == target_ref[...]).astype(jnp.bfloat16)

    packed = jnp.dot(onehot[...], x_ref[...], preferred_element_type=jnp.float32).astype(jnp.bfloat16)
    part = onehot.shape[0] // len(outs)
    for k, out in enumerate(outs):
        out[...] = packed[k * part : (k + 1) * part]


def pack(target, x, first, part, parts):
    rows, width = x.shape
    tile = 512
    return pl.pallas_call(
        functools.partial(pack_kernel, first),
        grid=(width // tile,),
        in_specs=[pl.BlockSpec((1, rows), lambda i: (0, 0)), pl.BlockSpec((rows, tile), lambda i: (0, i))],
        out_specs=[pl.BlockSpec((part, tile), lambda i: (0, i))] * parts,
        out_shape=[jax.ShapeDtypeStruct((part, width), x.dtype)] * parts,
        scratch_shapes=[pltpu.VMEM((part * parts, rows), jnp.bfloat16)],
        compiler_params=params(),
        cost_estimate=cost(2 * part * parts * rows * width, 2 * (rows + part * parts) * width),
        name="pack_rows",
    )(target, x)


def project_kernel(place_ref, x_ref, w_ref, o_ref):
    o_ref[...] = jnp.dot(x_ref[...], w_ref[...], preferred_element_type=jnp.float32).astype(o_ref.dtype)


def project(half, x, w):
    rows, width = x.shape
    columns = w.shape[1] // 2
    tile = 256
    steps = columns // tile
    return pl.pallas_call(
        project_kernel,
        grid_spec=pltpu.PrefetchScalarGridSpec(
            num_scalar_prefetch=1,
            grid=(steps,),
            in_specs=[
                pl.BlockSpec((rows, width), lambda i, place: (0, 0)),
                pl.BlockSpec((width, tile), lambda i, place: (0, place[0] * steps + i)),
            ],
            out_specs=pl.BlockSpec((rows, tile), lambda i, place: (0, i)),
        ),
        out_shape=jax.ShapeDtypeStruct((rows, columns), jnp.bfloat16),
        compiler_params=params(),
        cost_estimate=cost(2 * rows * width * columns, 2 * (rows * width + columns * width + rows * columns)),
        name="project_half",
    )(half.reshape(1), x, w)


def spans(arrays):
    ends, start = [], 0
    for array in arrays:
        ends.append((start, start + array.shape[0]))
        start += array.shape[0]
    return ends


def picked(start, end):
    return lambda i: (jnp.clip(i - start, 0, end - start - 1), 0, 0)


def down_kernel(ranges, *refs):
    xs, ws, o_ref = refs[: -1 - len(ranges)], refs[-1 - len(ranges) : -1], refs[-1]
    step = pl.program_id(0)
    rows = jnp.concatenate([x[...] for x in xs], axis=0)
    for w_ref, (start, end) in zip(ws, ranges):

        @pl.when((step >= start) & (step < end))
        def _():
            o_ref[...] = lax.dot_general(rows, w_ref[...], NT, preferred_element_type=jnp.float32)


def down(xs, ws):
    ranges = spans(ws)
    adapters, (_, rank, width) = ranges[-1][1], ws[0].shape
    rows = len(xs) * MOST
    return pl.pallas_call(
        functools.partial(down_kernel, ranges),
        grid=(adapters,),
        in_specs=[pl.BlockSpec((MOST, width), lambda i: (i, 0))] * len(xs)
        + [pl.BlockSpec((None, rank, width), picked(*span)) for span in ranges],
        out_specs=pl.BlockSpec((None, rows, rank), lambda i: (i, 0, 0)),
        out_shape=jax.ShapeDtypeStruct((adapters, rows, rank), jnp.float32),
        compiler_params=params(),
        cost_estimate=cost(2 * adapters * rows * rank * width, 2 * adapters * width * (rank + rows)),
        name="down_rows",
    )(*xs, *ws)


def lift_kernel(ranges, y_ref, *refs):
    us, outs = refs[: len(ranges)], refs[len(ranges) :]
    step = pl.program_id(0)
    for u_ref, (start, end) in zip(us, ranges):

        @pl.when((step >= start) & (step < end))
        def _():
            rows = jnp.dot(y_ref[...], u_ref[...], preferred_element_type=jnp.float32).astype(jnp.bfloat16)
            for k, out in enumerate(outs):
                out[...] = rows[k * MOST : (k + 1) * MOST]


def lift(y, us):
    ranges = spans(us)
    adapters, rows, rank = y.shape
    columns = us[0].shape[2]
    parts = rows // MOST
    return pl.pallas_call(
        functools.partial(lift_kernel, ranges),
        grid=(adapters,),
        in_specs=[pl.BlockSpec((None, rows, rank), lambda i: (i, 0, 0))]
        + [pl.BlockSpec((None, rank, columns), picked(*span)) for span in ranges],
        out_specs=[pl.BlockSpec((MOST, columns), lambda i: (i, 0))] * parts,
        out_shape=[jax.ShapeDtypeStruct((adapters * MOST, columns), jnp.bfloat16)] * parts,
        compiler_params=params(),
        cost_estimate=cost(2 * adapters * rows * rank * columns, 2 * adapters * columns * (rank + rows)),
        name="lift_rows",
    )(y, *us)


def finish_kernel(target_ref, own_ref, other_ref, *rest):
    pieces, o_ref, onehot = rest[:-2], rest[-2], rest[-1]

    @pl.when(pl.program_id(0) == 0)
    def _():
        place = lax.broadcasted_iota(jnp.int32, onehot.shape, 1)
        onehot[...] = (place == target_ref[...]).astype(jnp.bfloat16)

    lifted = jnp.concatenate([piece[...] for piece in pieces], axis=0)
    total = jnp.dot(onehot[...], lifted, preferred_element_type=jnp.float32)
    base = own_ref[...].astype(jnp.float32) + other_ref[...].astype(jnp.float32)
    o_ref[...] = (base + total).astype(o_ref.dtype)


def finish(target, own, other, pieces):
    rows, columns = own.shape
    tile = 512
    places = sum(piece.shape[0] for piece in pieces)
    return pl.pallas_call(
        finish_kernel,
        grid=(columns // tile,),
        in_specs=[pl.BlockSpec((rows, 1), lambda i: (0, 0))]
        + [pl.BlockSpec((rows, tile), lambda i: (0, i))] * 2
        + [pl.BlockSpec((piece.shape[0], tile), lambda i: (0, i)) for piece in pieces],
        out_specs=pl.BlockSpec((rows, tile), lambda i: (0, i)),
        out_shape=jax.ShapeDtypeStruct((rows, columns), jnp.bfloat16),
        scratch_shapes=[pltpu.VMEM((rows, places), jnp.bfloat16)],
        compiler_params=params(),
        cost_estimate=cost(2 * rows * places * columns, 8 * rows * columns),
        name="finish_rows",
    )(target, own, other, *pieces)


def places(request_adapter, adapter_slot, total):
    rows = request_adapter.shape[0]
    ids = request_adapter[:, 0]
    names = lax.broadcasted_iota(jnp.int32, (rows, total), 1)
    slots = jnp.sum(jnp.where(ids[:, None] == names, adapter_slot[None, :], 0), axis=1)
    onehot = (slots[:, None] == names).astype(jnp.bfloat16)
    row_iota = lax.broadcasted_iota(jnp.int32, (rows, rows), 0)
    col_iota = lax.broadcasted_iota(jnp.int32, (rows, rows), 1)
    earlier = (row_iota > col_iota).astype(jnp.bfloat16)
    counts = jnp.dot(earlier, onehot, preferred_element_type=jnp.float32)
    position = jnp.sum(counts * onehot.astype(jnp.float32), axis=1).astype(jnp.int32)
    return slots, position


def after(x, *earlier):
    return lax.optimization_barrier((x, *earlier))[0]


def by_planes(hidden_input, query_weight, slot_down_weight, slot_up_weight, request_adapter, adapter_slot):
    owned = slot_down_weight.shape[0]
    cut = owned // 2
    served = 2 * owned + cut
    rest = 4 * owned - served
    me = lax.axis_index("rep")
    plane, column = me // COLUMNS, me % COLUMNS
    inner = (plane == 1) | (plane == 2)
    every = range(COLUMNS * PLANES)
    inside = [r for r in every if r // COLUMNS in (1, 2)]
    outside = [r for r in every if r // COLUMNS in (0, 3)]

    def send(x, pairs, *earlier):
        return lax.ppermute(after(x, *earlier) if earlier else x, "rep", pairs)

    pair = [(r, r ^ 4) for r in every]
    across = [(r, r ^ 12) for r in inside]
    outward = [(r, r ^ 4) for r in inside]
    inward = [(r, r ^ 4) for r in outside]
    turn = [[(r, r ^ d) for r in every] for d in range(COLUMNS)]

    slots, position = places(request_adapter, adapter_slot, owned * COLUMNS * PLANES)
    slot_plane = slots // (owned * COLUMNS)
    slot_column = slots // owned % COLUMNS
    other = slot_plane // 2 != plane // 2
    second = jnp.where(other, (slot_plane == 0) | (slot_plane == 3), slot_plane != plane)
    number = (2 * other.astype(jnp.int32) + second.astype(jnp.int32)) * owned + slots % owned
    turned = slot_column ^ column
    there = (turned * rest + number - served) * MOST
    here = (COLUMNS * rest + turned * served + number) * MOST
    target = jnp.where(number < served, here, there) + position

    down_own = jnp.swapaxes(slot_down_weight, 1, 2)
    up_own = slot_up_weight
    down_pair = send(down_own, pair)
    down_near = send(down_own, across)

    away = pack(target[None, :], hidden_input, 0, rest * MOST, COLUMNS)
    home = pack(target[None, :], hidden_input, COLUMNS * rest * MOST, served * MOST, COLUMNS)
    away = [away[0]] + [send(away[d], turn[d]) for d in range(1, COLUMNS)]

    up_pair = send(up_own, pair, down_pair)
    up_near = send(up_own, across, down_near)
    beside = [home[0]] + [send(home[d], turn[d], away[1], away[2]) for d in (1, 2)]
    beside.append(send(home[3], turn[3], away[3], beside[1]))

    down_out = send(down_near[:cut], outward, up_pair)
    up_far = send(up_pair, across, up_near)
    moved, last = [], up_pair
    for rows in away:
        last = send(rows, inward, last)
        moved.append(last)
    down_far = send(down_pair, across, up_far)
    up_near_out = send(up_near, outward, down_out)
    up_far_out = send(up_far, outward, up_near_out)
    down_part = jnp.where(inner, down_near[:cut], down_out)
    up_near = jnp.where(inner, up_near, up_near_out)
    up_far = jnp.where(inner, up_far, up_far_out)

    tp = lax.axis_index("tp")
    given = project(1 - tp, hidden_input, query_weight)
    base_other = lax.ppermute(given, "tp", SWAP)
    base_own = project(tp, hidden_input, query_weight)

    def both(y):
        return (y + lax.ppermute(y, "tp", SWAP)).astype(jnp.bfloat16)

    low = both(down(beside, [down_own, down_pair, down_part]))
    rows = lift(low, [up_own, up_pair, up_near[:cut]])
    lifted = [rows[0]] + [send(rows[d], turn[d]) for d in range(1, COLUMNS)]

    half = COLUMNS * MOST
    low = both(down(away + moved, [down_near[cut:], down_far]))
    low = jnp.where(inner, low[:, :half], send(low[:, half:], outward))
    rows = lift(low, [up_near[cut:], up_far])
    lifted = [rows[0]] + [send(rows[d], turn[d]) for d in range(1, COLUMNS)] + lifted
    return finish(target[:, None], base_own, base_other, lifted)


def by_gather(hidden_input, query_weight, slot_down_weight, slot_up_weight, request_adapter, adapter_slot):
    local_width = hidden_input.shape[1]
    output_width = slot_up_weight.shape[2]
    total = slot_down_weight.shape[0] * lax.axis_size("rep")
    base_sum = lax.psum_scatter(
        lax.dot_general(
            query_weight, hidden_input, (((0,), (1,)), ((), ())), preferred_element_type=jnp.float32
        ).astype(jnp.bfloat16),
        "tp",
        scatter_dimension=0,
        tiled=True,
    ).astype(jnp.float32)
    slots, position = places(request_adapter, adapter_slot, total)
    target = slots * MOST + position
    buffer = jnp.zeros((total * MOST, local_width), jnp.bfloat16).at[target].set(hidden_input)
    slot_rows = buffer.reshape(total, MOST, local_width)
    lowered = jnp.einsum(
        "amd,adr->amr",
        slot_rows,
        lax.all_gather(slot_down_weight, "rep", axis=0, tiled=True),
        preferred_element_type=jnp.float32,
    )
    lowered = lax.psum(lowered.astype(jnp.bfloat16), "tp")
    lifted = jnp.einsum(
        "amr,are->ame",
        lowered,
        lax.all_gather(slot_up_weight, "rep", axis=0, tiled=True),
        preferred_element_type=jnp.float32,
    )
    lift_rows = lifted.astype(jnp.bfloat16).reshape(total * MOST, output_width)[target]
    return (base_sum.T + lift_rows.astype(jnp.float32)).astype(jnp.bfloat16)


def solution(mesh):
    in_specs = (
        P("rep", "tp"),
        P("tp", None),
        P("rep", "tp", None),
        P("rep", None, "tp"),
        P("rep", None),
        P(),
    )
    out_specs = P("rep", "tp")
    planes = mesh.shape["rep"] == COLUMNS * PLANES and mesh.shape["tp"] == 2
    shards = by_planes if planes else by_gather
    return jax.shard_map(shards, mesh=mesh, in_specs=in_specs, out_specs=out_specs, check_vma=False)
```

```python
import functools

import jax
import jax.numpy as jnp
from jax import lax
from jax.experimental import pallas as pl
from jax.experimental.pallas import tpu as pltpu
from jax.sharding import PartitionSpec as P

MOST = 16
COLUMNS = 4
PLANES = 4
SWAP = [(0, 1), (1, 0)]
LIMIT = 56 * 1024 * 1024
NT = (((1,), (1,)), ((), ()))


def params(steps=1):
    return pltpu.CompilerParams(dimension_semantics=("arbitrary",) * steps, vmem_limit_bytes=LIMIT)


def cost(flops, size):
    return pl.CostEstimate(flops=flops, bytes_accessed=size, transcendentals=0)


def pack_kernel(first, target_ref, x_ref, *rest):
    outs, onehot = rest[:-1], rest[-1]

    @pl.when(pl.program_id(0) == 0)
    def _():
        place = lax.broadcasted_iota(jnp.int32, onehot.shape, 0) + first
        onehot[...] = (place == target_ref[...]).astype(jnp.bfloat16)

    packed = jnp.dot(onehot[...], x_ref[...], preferred_element_type=jnp.float32).astype(jnp.bfloat16)
    part = onehot.shape[0] // len(outs)
    for k, out in enumerate(outs):
        out[...] = packed[k * part : (k + 1) * part]


def pack(target, x, first, part, parts):
    rows, width = x.shape
    tile = 1024
    return pl.pallas_call(
        functools.partial(pack_kernel, first),
        grid=(width // tile,),
        in_specs=[pl.BlockSpec((1, rows), lambda i: (0, 0)), pl.BlockSpec((rows, tile), lambda i: (0, i))],
        out_specs=[pl.BlockSpec((part, tile), lambda i: (0, i))] * parts,
        out_shape=[jax.ShapeDtypeStruct((part, width), x.dtype)] * parts,
        scratch_shapes=[pltpu.VMEM((part * parts, rows), jnp.bfloat16)],
        compiler_params=params(),
        cost_estimate=cost(2 * part * parts * rows * width, 2 * (rows + part * parts) * width),
        name="pack_rows",
    )(target, x)


def project_kernel(place_ref, x_ref, w_ref, o_ref):
    o_ref[...] = jnp.dot(x_ref[...], w_ref[...], preferred_element_type=jnp.float32).astype(o_ref.dtype)


def project(half, x, w):
    rows, width = x.shape
    columns = w.shape[1] // 2
    tile = 256
    steps = columns // tile
    return pl.pallas_call(
        project_kernel,
        grid_spec=pltpu.PrefetchScalarGridSpec(
            num_scalar_prefetch=1,
            grid=(steps,),
            in_specs=[
                pl.BlockSpec((rows, width), lambda i, place: (0, 0)),
                pl.BlockSpec((width, tile), lambda i, place: (0, place[0] * steps + i)),
            ],
            out_specs=pl.BlockSpec((rows, tile), lambda i, place: (0, i)),
        ),
        out_shape=jax.ShapeDtypeStruct((rows, columns), jnp.bfloat16),
        compiler_params=params(),
        cost_estimate=cost(2 * rows * width * columns, 2 * (rows * width + columns * width + rows * columns)),
        name="project_half",
    )(half.reshape(1), x, w)


def factor_specs(groups, rank, tile):
    specs = []
    for arrays, first, count in groups:
        shape = (count, rank, tile)
        specs += [pl.BlockSpec(shape, lambda k, at=first // count: (at, 0, k))] * len(arrays)
    return specs


def factors(refs, groups):
    at = start = 0
    for held, count in groups:
        total = functools.reduce(jnp.add, [ref[...] for ref in refs[at : at + held]])
        yield start, count, total.reshape(count * total.shape[1], total.shape[2])
        at += held
        start += count


def flat(groups):
    return [array for arrays, _, _ in groups for array in arrays]


def shape_of(groups):
    return [(len(arrays), count) for arrays, _, count in groups]


def down_kernel(groups, sources, *refs):
    xs, ws, o_ref = refs[:sources], refs[sources:-1], refs[-1]
    step = pl.program_id(0)
    sides = sources // COLUMNS
    side_rows = o_ref.shape[0] // sides

    @pl.when(step == 0)
    def _():
        o_ref[...] = jnp.zeros_like(o_ref)

    for start, count, w in factors(ws, groups):
        rank = w.shape[0] // count
        rows = jnp.concatenate([x[start * MOST : (start + count) * MOST] for x in xs], axis=0)
        y = lax.dot_general(rows, w, NT, preferred_element_type=jnp.float32)
        owner = lax.broadcasted_iota(jnp.int32, y.shape, 0) // MOST % count
        y = jnp.where(owner == lax.broadcasted_iota(jnp.int32, y.shape, 1) // rank, y, 0.0)
        part = COLUMNS * count * MOST
        for side in range(sides):
            at = side * side_rows + start * COLUMNS * MOST
            o_ref[at : at + part, : w.shape[0]] += y[side * part : (side + 1) * part]


def down(xs, groups):
    served = sum(count for _, _, count in groups)
    _, rank, width = groups[0][0][0].shape
    tile = 1024
    rows = len(xs) * served * MOST
    wide = max(count for _, _, count in groups) * rank

    def block(section):
        return pl.BlockSpec((served * MOST, tile), lambda k: (section, k))

    return pl.pallas_call(
        functools.partial(down_kernel, shape_of(groups), len(xs)),
        grid=(width // tile,),
        in_specs=[block(section) for _, section in xs] + factor_specs(groups, rank, tile),
        out_specs=pl.BlockSpec((rows, wide), lambda k: (0, 0)),
        out_shape=jax.ShapeDtypeStruct((rows, wide), jnp.float32),
        compiler_params=params(),
        cost_estimate=cost(2 * rows * wide * width, 2 * width * (served * rank + rows)),
        name="down_rows",
    )(*[x for x, _ in xs], *flat(groups))


def lift_kernel(groups, count_y, *refs):
    outs, y = refs[-1 - COLUMNS : -1], refs[-1]
    ys, us = refs[:count_y], refs[count_y : -1 - COLUMNS]

    @pl.when(pl.program_id(0) == 0)
    def _():
        y[...] = functools.reduce(jnp.add, [ref[...] for ref in ys]).astype(jnp.bfloat16)

    for start, count, u in factors(us, groups):
        part = count * MOST
        at = start * COLUMNS * MOST
        low = y[at : at + COLUMNS * part, : u.shape[0]]
        rows = jnp.dot(low, u, preferred_element_type=jnp.float32).astype(jnp.bfloat16)
        for k, out in enumerate(outs):
            out[start * MOST : start * MOST + part] = rows[k * part : (k + 1) * part]


def lift(ys, groups):
    served = sum(count for _, _, count in groups)
    _, rank, columns = groups[0][0][0].shape
    tile = 512
    rows, wide = served * COLUMNS * MOST, ys[0].shape[1]
    return pl.pallas_call(
        functools.partial(lift_kernel, shape_of(groups), len(ys)),
        grid=(columns // tile,),
        in_specs=[pl.BlockSpec((rows, wide), lambda k: (0, 0))] * len(ys) + factor_specs(groups, rank, tile),
        out_specs=[pl.BlockSpec((served * MOST, tile), lambda k: (0, k))] * COLUMNS,
        out_shape=[jax.ShapeDtypeStruct((served * MOST, columns), jnp.bfloat16)] * COLUMNS,
        scratch_shapes=[pltpu.VMEM((rows, wide), jnp.bfloat16)],
        compiler_params=params(),
        cost_estimate=cost(2 * rows * wide * columns, 2 * columns * (served * rank + rows)),
        name="lift_rows",
    )(*ys, *flat(groups))


def finish_kernel(count, onehot_ref, *rest):
    bases, pieces, o_ref = rest[:count], rest[count:-1], rest[-1]
    lifted = jnp.concatenate([piece[...] for piece in pieces], axis=0)
    total = jnp.dot(onehot_ref[...], lifted, preferred_element_type=jnp.float32)
    for base in bases:
        total += base[...].astype(jnp.float32)
    o_ref[...] = total.astype(o_ref.dtype)


def finish(onehot, bases, pieces, dtype):
    rows, columns = bases[0].shape
    tile = 512
    held = onehot.shape[1]
    return pl.pallas_call(
        functools.partial(finish_kernel, len(bases)),
        grid=(columns // tile,),
        in_specs=[pl.BlockSpec((rows, held), lambda i: (0, 0))]
        + [pl.BlockSpec((rows, tile), lambda i: (0, i)) for _ in bases]
        + [pl.BlockSpec((piece.shape[0], tile), lambda i: (0, i)) for piece in pieces],
        out_specs=pl.BlockSpec((rows, tile), lambda i: (0, i)),
        out_shape=jax.ShapeDtypeStruct((rows, columns), dtype),
        compiler_params=params(),
        cost_estimate=cost(2 * rows * held * columns, 8 * rows * columns),
        name="finish_rows",
    )(onehot, *bases, *pieces)


def join_kernel(*refs):
    pieces, o_ref = refs[:-1], refs[-1]
    rows = pieces[0].shape[0]
    for k, piece in enumerate(pieces):
        o_ref[k * rows : (k + 1) * rows] = piece[...]


def join(pieces):
    rows, width = pieces[0].shape
    tile = 1024
    return pl.pallas_call(
        join_kernel,
        grid=(width // tile,),
        in_specs=[pl.BlockSpec((rows, tile), lambda k: (0, k))] * len(pieces),
        out_specs=pl.BlockSpec((rows * len(pieces), tile), lambda k: (0, k)),
        out_shape=jax.ShapeDtypeStruct((rows * len(pieces), width), pieces[0].dtype),
        compiler_params=params(),
        cost_estimate=cost(0, 4 * rows * len(pieces) * width),
        name="join_rows",
    )(*pieces)


def places(request_adapter, adapter_slot, total):
    rows = request_adapter.shape[0]
    ids = request_adapter[:, 0]
    names = lax.broadcasted_iota(jnp.int32, (rows, total), 1)
    slots = jnp.sum(jnp.where(ids[:, None] == names, adapter_slot[None, :], 0), axis=1)
    onehot = (slots[:, None] == names).astype(jnp.bfloat16)
    row_iota = lax.broadcasted_iota(jnp.int32, (rows, rows), 0)
    col_iota = lax.broadcasted_iota(jnp.int32, (rows, rows), 1)
    earlier = (row_iota > col_iota).astype(jnp.bfloat16)
    counts = jnp.dot(earlier, onehot, preferred_element_type=jnp.float32)
    position = jnp.sum(counts * onehot.astype(jnp.float32), axis=1).astype(jnp.int32)
    return slots, position


def after(x, *earlier):
    return lax.optimization_barrier((x, *earlier))[0]


def by_planes(hidden_input, query_weight, slot_down_weight, slot_up_weight, request_adapter, adapter_slot):
    owned = slot_down_weight.shape[0]
    cut = owned // 2
    served = 2 * owned + cut
    rest = 4 * owned - served
    me = lax.axis_index("rep")
    plane, column = me // COLUMNS, me % COLUMNS
    every = range(COLUMNS * PLANES)
    inside = [r for r in every if r // COLUMNS in (1, 2)]
    outside = [r for r in every if r // COLUMNS in (0, 3)]

    def send(x, pairs, *earlier):
        return lax.ppermute(after(x, *earlier) if earlier else x, "rep", pairs)

    pair = [(r, r ^ 4) for r in every]
    across = [(r, r ^ 12) for r in inside]
    outward = [(r, r ^ 4) for r in inside]
    inward = [(r, r ^ 4) for r in outside]
    turn = [[(r, r ^ d) for r in every] for d in range(COLUMNS)]

    slots, position = places(request_adapter, adapter_slot, owned * COLUMNS * PLANES)
    slot_plane = slots // (owned * COLUMNS)
    slot_column = slots // owned % COLUMNS
    other = slot_plane // 2 != plane // 2
    second = jnp.where(other, (slot_plane == 0) | (slot_plane == 3), slot_plane != plane)
    number = (2 * other.astype(jnp.int32) + second.astype(jnp.int32)) * owned + slots % owned
    turned = slot_column ^ column
    there = (turned * rest + number - served) * MOST
    here = (COLUMNS * rest + turned * served + number) * MOST
    target = jnp.where(number < served, here, there) + position

    down_own = jnp.swapaxes(slot_down_weight, 1, 2)
    up_own = slot_up_weight
    tp = lax.axis_index("tp")
    down_pair = send(down_own, pair)
    down_near = send(down_own, across)

    split = COLUMNS * rest * MOST
    away = pack(target[None, :], hidden_input, 0, rest * MOST, COLUMNS)
    home = pack(target[None, :], after(hidden_input, away[0]), split, served * MOST, COLUMNS)
    spots = lax.broadcasted_iota(jnp.int32, (target.shape[0], 4 * owned * COLUMNS * MOST), 1)
    onehot = (target[:, None] == spots).astype(jnp.bfloat16)
    back_away, back_home = onehot[:, :split], onehot[:, split:]
    away = [away[0]] + [send(away[d], turn[d]) for d in range(1, COLUMNS)]
    given = project(1 - tp, after(hidden_input, home[0], back_away, back_home), query_weight)

    up_pair = send(up_own, pair, down_pair, given)
    up_near = send(up_own, across, down_near, given)
    beside = [home[0]] + [send(home[d], turn[d], away[d], given) for d in (1, 2)]
    moving = join(away)
    base_own = project(tp, after(hidden_input, down_pair, down_near, moving), query_weight)

    moved = send(moving, inward, up_pair, beside[1], beside[2], base_own)
    down_out = send(down_near[:cut], outward, up_pair, base_own)
    up_far = send(up_pair, across, up_near, base_own)
    beside.append(send(home[3], turn[3], beside[1], beside[2], base_own))
    down_far = send(down_pair, across, up_far, down_out)
    up_near_out = send(up_near, outward, down_out)
    base_other = lax.ppermute(after(given, beside[3]), "tp", SWAP)

    def swapped(y):
        return lax.ppermute(y, "tp", SWAP)

    low = down(
        [(rows, 0) for rows in beside],
        [([down_own], 0, owned), ([down_pair], 0, owned), ([down_near, down_out], 0, cut)],
    )
    up_far_out = send(up_far, outward, up_near_out, low)
    rows = lift(
        [low, swapped(low)], [([up_own], 0, owned), ([up_pair], 0, owned), ([up_near, up_near_out], 0, cut)]
    )
    lifted_home = [rows[0]] + [send(rows[d], turn[d]) for d in range(1, COLUMNS)]

    low = down(
        [(after(away[0], up_far_out, rows[0]), 0)] + [(rows, 0) for rows in away[1:]] + [(moved, d) for d in range(COLUMNS)],
        [([down_near], cut, owned - cut), ([down_far], 0, owned)],
    )
    low = (low + swapped(low)).astype(jnp.bfloat16)
    rows = lift(
        [low, send(low[low.shape[0] // 2 :], outward)],
        [([up_near, up_near_out], cut, owned - cut), ([up_far, up_far_out], 0, owned)],
    )
    lifted_away = [rows[0]] + [send(rows[d], turn[d]) for d in range(1, COLUMNS)]
    part = finish(back_home, [after(base_own, rows[0]), base_other], lifted_home, jnp.float32)
    return finish(back_away, [part], lifted_away, jnp.bfloat16)


def by_gather(hidden_input, query_weight, slot_down_weight, slot_up_weight, request_adapter, adapter_slot):
    local_width = hidden_input.shape[1]
    output_width = slot_up_weight.shape[2]
    total = slot_down_weight.shape[0] * lax.axis_size("rep")
    base_sum = lax.psum_scatter(
        lax.dot_general(
            query_weight, hidden_input, (((0,), (1,)), ((), ())), preferred_element_type=jnp.float32
        ).astype(jnp.bfloat16),
        "tp",
        scatter_dimension=0,
        tiled=True,
    ).astype(jnp.float32)
    slots, position = places(request_adapter, adapter_slot, total)
    target = slots * MOST + position
    buffer = jnp.zeros((total * MOST, local_width), jnp.bfloat16).at[target].set(hidden_input)
    slot_rows = buffer.reshape(total, MOST, local_width)
    lowered = jnp.einsum(
        "amd,adr->amr",
        slot_rows,
        lax.all_gather(slot_down_weight, "rep", axis=0, tiled=True),
        preferred_element_type=jnp.float32,
    )
    lowered = lax.psum(lowered.astype(jnp.bfloat16), "tp")
    lifted = jnp.einsum(
        "amr,are->ame",
        lowered,
        lax.all_gather(slot_up_weight, "rep", axis=0, tiled=True),
        preferred_element_type=jnp.float32,
    )
    lift_rows = lifted.astype(jnp.bfloat16).reshape(total * MOST, output_width)[target]
    return (base_sum.T + lift_rows.astype(jnp.float32)).astype(jnp.bfloat16)


def solution(mesh):
    in_specs = (
        P("rep", "tp"),
        P("tp", None),
        P("rep", "tp", None),
        P("rep", None, "tp"),
        P("rep", None),
        P(),
    )
    out_specs = P("rep", "tp")
    planes = mesh.shape["rep"] == COLUMNS * PLANES and mesh.shape["tp"] == 2
    shards = by_planes if planes else by_gather
    return jax.shard_map(shards, mesh=mesh, in_specs=in_specs, out_specs=out_specs, check_vma=False)
```

```python
import functools

import jax
import jax.numpy as jnp
from jax import lax
from jax.experimental import pallas as pl
from jax.experimental.pallas import tpu as pltpu
from jax.sharding import PartitionSpec as P

MOST = 16
COLUMNS = 4
PLANES = 4
SWAP = [(0, 1), (1, 0)]
LIMIT = 56 * 1024 * 1024
NT = (((1,), (1,)), ((), ()))


def params(steps=1):
    return pltpu.CompilerParams(dimension_semantics=("arbitrary",) * steps, vmem_limit_bytes=LIMIT)


def cost(flops, size):
    return pl.CostEstimate(flops=flops, bytes_accessed=size, transcendentals=0)


def pack_kernel(first, target_ref, x_ref, *rest):
    outs, onehot = rest[:-1], rest[-1]

    @pl.when(pl.program_id(0) == 0)
    def _():
        place = lax.broadcasted_iota(jnp.int32, onehot.shape, 0) + first
        onehot[...] = (place == target_ref[...]).astype(jnp.bfloat16)

    packed = jnp.dot(onehot[...], x_ref[...], preferred_element_type=jnp.float32).astype(jnp.bfloat16)
    part = onehot.shape[0] // len(outs)
    for k, out in enumerate(outs):
        out[...] = packed[k * part : (k + 1) * part]


def pack(target, x, first, part, parts):
    rows, width = x.shape
    tile = 1024
    return pl.pallas_call(
        functools.partial(pack_kernel, first),
        grid=(width // tile,),
        in_specs=[pl.BlockSpec((1, rows), lambda i: (0, 0)), pl.BlockSpec((rows, tile), lambda i: (0, i))],
        out_specs=[pl.BlockSpec((part, tile), lambda i: (0, i))] * parts,
        out_shape=[jax.ShapeDtypeStruct((part, width), x.dtype)] * parts,
        scratch_shapes=[pltpu.VMEM((part * parts, rows), jnp.bfloat16)],
        compiler_params=params(),
        cost_estimate=cost(2 * part * parts * rows * width, 2 * (rows + part * parts) * width),
        name="pack_rows",
    )(target, x)


def project_kernel(place_ref, x_ref, w_ref, o_ref):
    o_ref[...] = jnp.dot(x_ref[...], w_ref[...], preferred_element_type=jnp.float32).astype(o_ref.dtype)


def project(half, x, w):
    rows, width = x.shape
    columns = w.shape[1] // 2
    tile = 256
    steps = columns // tile
    return pl.pallas_call(
        project_kernel,
        grid_spec=pltpu.PrefetchScalarGridSpec(
            num_scalar_prefetch=1,
            grid=(steps,),
            in_specs=[
                pl.BlockSpec((rows, width), lambda i, place: (0, 0)),
                pl.BlockSpec((width, tile), lambda i, place: (0, place[0] * steps + i)),
            ],
            out_specs=pl.BlockSpec((rows, tile), lambda i, place: (0, i)),
        ),
        out_shape=jax.ShapeDtypeStruct((rows, columns), jnp.bfloat16),
        compiler_params=params(),
        cost_estimate=cost(2 * rows * width * columns, 2 * (rows * width + columns * width + rows * columns)),
        name="project_half",
    )(half.reshape(1), x, w)


def factor_specs(groups, rank, tile):
    specs = []
    for arrays, first, count in groups:
        shape = (count, rank, tile)
        specs += [pl.BlockSpec(shape, lambda k, at=first // count: (at, 0, k))] * len(arrays)
    return specs


def factors(refs, groups):
    at = start = 0
    for held, count in groups:
        total = functools.reduce(jnp.add, [ref[...] for ref in refs[at : at + held]])
        yield start, count, total.reshape(count * total.shape[1], total.shape[2])
        at += held
        start += count


def flat(groups):
    return [array for arrays, _, _ in groups for array in arrays]


def shape_of(groups):
    return [(len(arrays), count) for arrays, _, count in groups]


def down_kernel(groups, sources, *refs):
    xs, ws, o_ref = refs[:sources], refs[sources:-1], refs[-1]
    step = pl.program_id(0)
    sides = sources // COLUMNS
    side_rows = o_ref.shape[0] // sides

    @pl.when(step == 0)
    def _():
        o_ref[...] = jnp.zeros_like(o_ref)

    for start, count, w in factors(ws, groups):
        rank = w.shape[0] // count
        rows = jnp.concatenate([x[start * MOST : (start + count) * MOST] for x in xs], axis=0)
        y = lax.dot_general(rows, w, NT, preferred_element_type=jnp.float32)
        owner = lax.broadcasted_iota(jnp.int32, y.shape, 0) // MOST % count
        y = jnp.where(owner == lax.broadcasted_iota(jnp.int32, y.shape, 1) // rank, y, 0.0)
        part = COLUMNS * count * MOST
        for side in range(sides):
            at = side * side_rows + start * COLUMNS * MOST
            o_ref[at : at + part, : w.shape[0]] += y[side * part : (side + 1) * part]


def down(xs, groups):
    served = sum(count for _, _, count in groups)
    _, rank, width = groups[0][0][0].shape
    tile = 1024
    rows = len(xs) * served * MOST
    wide = max(count for _, _, count in groups) * rank

    def block(section):
        return pl.BlockSpec((served * MOST, tile), lambda k: (section, k))

    return pl.pallas_call(
        functools.partial(down_kernel, shape_of(groups), len(xs)),
        grid=(width // tile,),
        in_specs=[block(section) for _, section in xs] + factor_specs(groups, rank, tile),
        out_specs=pl.BlockSpec((rows, wide), lambda k: (0, 0)),
        out_shape=jax.ShapeDtypeStruct((rows, wide), jnp.float32),
        compiler_params=params(),
        cost_estimate=cost(2 * rows * wide * width, 2 * width * (served * rank + rows)),
        name="down_rows",
    )(*[x for x, _ in xs], *flat(groups))


def lift_kernel(groups, count_y, *refs):
    outs, y = refs[-1 - COLUMNS : -1], refs[-1]
    ys, us = refs[:count_y], refs[count_y : -1 - COLUMNS]

    @pl.when(pl.program_id(0) == 0)
    def _():
        y[...] = functools.reduce(jnp.add, [ref[...] for ref in ys]).astype(jnp.bfloat16)

    for start, count, u in factors(us, groups):
        part = count * MOST
        at = start * COLUMNS * MOST
        low = y[at : at + COLUMNS * part, : u.shape[0]]
        rows = jnp.dot(low, u, preferred_element_type=jnp.float32).astype(jnp.bfloat16)
        for k, out in enumerate(outs):
            out[start * MOST : start * MOST + part] = rows[k * part : (k + 1) * part]


def lift(ys, groups):
    served = sum(count for _, _, count in groups)
    _, rank, columns = groups[0][0][0].shape
    tile = 512
    rows, wide = served * COLUMNS * MOST, ys[0].shape[1]
    return pl.pallas_call(
        functools.partial(lift_kernel, shape_of(groups), len(ys)),
        grid=(columns // tile,),
        in_specs=[pl.BlockSpec((rows, wide), lambda k: (0, 0))] * len(ys) + factor_specs(groups, rank, tile),
        out_specs=[pl.BlockSpec((served * MOST, tile), lambda k: (0, k))] * COLUMNS,
        out_shape=[jax.ShapeDtypeStruct((served * MOST, columns), jnp.bfloat16)] * COLUMNS,
        scratch_shapes=[pltpu.VMEM((rows, wide), jnp.bfloat16)],
        compiler_params=params(),
        cost_estimate=cost(2 * rows * wide * columns, 2 * columns * (served * rank + rows)),
        name="lift_rows",
    )(*ys, *flat(groups))


def finish_kernel(count, onehot_ref, *rest):
    bases, pieces, o_ref = rest[:count], rest[count:-1], rest[-1]
    lifted = jnp.concatenate([piece[...] for piece in pieces], axis=0)
    total = jnp.dot(onehot_ref[...], lifted, preferred_element_type=jnp.float32)
    for base in bases:
        total += base[...].astype(jnp.float32)
    o_ref[...] = total.astype(o_ref.dtype)


def finish(onehot, bases, pieces, dtype):
    rows, columns = bases[0].shape
    tile = 512
    held = onehot.shape[1]
    return pl.pallas_call(
        functools.partial(finish_kernel, len(bases)),
        grid=(columns // tile,),
        in_specs=[pl.BlockSpec((rows, held), lambda i: (0, 0))]
        + [pl.BlockSpec((rows, tile), lambda i: (0, i)) for _ in bases]
        + [pl.BlockSpec((piece.shape[0], tile), lambda i: (0, i)) for piece in pieces],
        out_specs=pl.BlockSpec((rows, tile), lambda i: (0, i)),
        out_shape=jax.ShapeDtypeStruct((rows, columns), dtype),
        compiler_params=params(),
        cost_estimate=cost(2 * rows * held * columns, 8 * rows * columns),
        name="finish_rows",
    )(onehot, *bases, *pieces)


def join_kernel(*refs):
    pieces, o_ref = refs[:-1], refs[-1]
    rows = pieces[0].shape[0]
    for k, piece in enumerate(pieces):
        o_ref[k * rows : (k + 1) * rows] = piece[...]


def join(pieces):
    rows, width = pieces[0].shape
    tile = 1024
    return pl.pallas_call(
        join_kernel,
        grid=(width // tile,),
        in_specs=[pl.BlockSpec((rows, tile), lambda k: (0, k))] * len(pieces),
        out_specs=pl.BlockSpec((rows * len(pieces), tile), lambda k: (0, k)),
        out_shape=jax.ShapeDtypeStruct((rows * len(pieces), width), pieces[0].dtype),
        compiler_params=params(),
        cost_estimate=cost(0, 4 * rows * len(pieces) * width),
        name="join_rows",
    )(*pieces)


def places(request_adapter, adapter_slot, total):
    rows = request_adapter.shape[0]
    ids = request_adapter[:, 0]
    names = lax.broadcasted_iota(jnp.int32, (rows, total), 1)
    slots = jnp.sum(jnp.where(ids[:, None] == names, adapter_slot[None, :], 0), axis=1)
    onehot = (slots[:, None] == names).astype(jnp.bfloat16)
    row_iota = lax.broadcasted_iota(jnp.int32, (rows, rows), 0)
    col_iota = lax.broadcasted_iota(jnp.int32, (rows, rows), 1)
    earlier = (row_iota > col_iota).astype(jnp.bfloat16)
    counts = jnp.dot(earlier, onehot, preferred_element_type=jnp.float32)
    position = jnp.sum(counts * onehot.astype(jnp.float32), axis=1).astype(jnp.int32)
    return slots, position


EARLIER = {"home": ["away"], "given": ["home", "onehots"], "up_pair": ["down_pair", "given"], "up_near": ["down_near", "given"], "home1": ["away1", "given"], "home2": ["away2", "given"], "base_own": ["down_pair", "down_near", "joined"], "moved": ["up_pair", "home1", "home2", "base_own"], "down_out": ["up_pair", "base_own"], "up_far": ["up_near", "base_own"], "home3": ["home1", "home2", "base_own"], "down_far": ["up_far", "down_out"], "up_near_out": ["down_out"], "base_other": ["low_away"], "up_far_out": ["up_near_out", "low_home"], "low_away": ["up_far_out", "lift_home1", "lift_home2"], "part": ["rows_away"], "lift_home3": ["lift_home1"]}


def after(x, *earlier):
    return lax.optimization_barrier((x, *earlier))[0]


def by_planes(hidden_input, query_weight, slot_down_weight, slot_up_weight, request_adapter, adapter_slot):
    owned = slot_down_weight.shape[0]
    cut = owned // 2
    served = 2 * owned + cut
    rest = 4 * owned - served
    me = lax.axis_index("rep")
    plane, column = me // COLUMNS, me % COLUMNS
    every = range(COLUMNS * PLANES)
    inside = [r for r in every if r // COLUMNS in (1, 2)]
    outside = [r for r in every if r // COLUMNS in (0, 3)]
    pair = [(r, r ^ 4) for r in every]
    across = [(r, r ^ 12) for r in inside]
    outward = [(r, r ^ 4) for r in inside]
    inward = [(r, r ^ 4) for r in outside]
    turn = [[(r, r ^ d) for r in every] for d in range(COLUMNS)]

    slots, position = places(request_adapter, adapter_slot, owned * COLUMNS * PLANES)
    slot_plane = slots // (owned * COLUMNS)
    slot_column = slots // owned % COLUMNS
    other = slot_plane // 2 != plane // 2
    second = jnp.where(other, (slot_plane == 0) | (slot_plane == 3), slot_plane != plane)
    number = (2 * other.astype(jnp.int32) + second.astype(jnp.int32)) * owned + slots % owned
    turned = slot_column ^ column
    there = (turned * rest + number - served) * MOST
    here = (COLUMNS * rest + turned * served + number) * MOST
    target = jnp.where(number < served, here, there) + position
    split = COLUMNS * rest * MOST
    spots = lax.broadcasted_iota(jnp.int32, (target.shape[0], 4 * owned * COLUMNS * MOST), 1)
    onehot = (target[:, None] == spots).astype(jnp.bfloat16)
    back_away, back_home = onehot[:, :split], onehot[:, split:]

    down_own = jnp.swapaxes(slot_down_weight, 1, 2)
    up_own = slot_up_weight
    tp = lax.axis_index("tp")
    made = {}

    def need(name):
        if name not in made:
            made[name] = steps[name](name)
        return made[name]

    def gate(name, x):
        earlier = [need(one) for one in EARLIER.get(name, ())]
        return after(x, *earlier) if earlier else x

    def send(pairs, what):
        return lambda name: lax.ppermute(gate(name, what()), "rep", pairs)

    def swap(what):
        return lambda name: lax.ppermute(gate(name, what()), "tp", SWAP)

    def packed(first, count):
        return lambda name: pack(target[None, :], gate(name, hidden_input), first, count * MOST, COLUMNS)

    def rows_away():
        return [need("away")[0]] + [need(f"away{d}") for d in (1, 2, 3)]

    def rows_home():
        return [need("home")[0]] + [need(f"home{d}") for d in (1, 2, 3)]

    def lower_home(name):
        factors = [([down_own], 0, owned), ([need("down_pair")], 0, owned)]
        factors.append(([need("down_near"), need("down_out")], 0, cut))
        first, *others = rows_home()
        return down([(rows, 0) for rows in (gate(name, first), *others)], factors)

    def lift_home(name):
        factors = [([up_own], 0, owned), ([need("up_pair")], 0, owned)]
        factors.append(([need("up_near"), need("up_near_out")], 0, cut))
        return lift([gate(name, need("low_home")), need("low_home_swap")], factors)

    def lower_away(name):
        first, *others = rows_away()
        xs = [(rows, 0) for rows in (gate(name, first), *others)] + [(need("moved"), d) for d in range(COLUMNS)]
        return down(xs, [([need("down_near")], cut, owned - cut), ([need("down_far")], 0, owned)])

    def lift_away(name):
        factors = [([need("up_near"), need("up_near_out")], cut, owned - cut)]
        factors.append(([need("up_far"), need("up_far_out")], 0, owned))
        return lift([gate(name, need("low_sum")), need("low_out")], factors)

    def sum_away(name):
        return (need("low_away") + need("low_away_swap")).astype(jnp.bfloat16)

    def finish_home(name):
        pieces = [need("rows_home")[0]] + [need(f"lift_home{d}") for d in (1, 2, 3)]
        return finish(back_home, [gate(name, need("base_own")), need("base_other")], pieces, jnp.float32)

    def finish_away(name):
        pieces = [need("rows_away")[0]] + [need(f"lift_away{d}") for d in (1, 2, 3)]
        return finish(back_away, [need("part")], pieces, jnp.bfloat16)

    steps = {
        "away": packed(0, rest),
        "home": packed(split, served),
        "given": lambda name: project(1 - tp, gate(name, hidden_input), query_weight),
        "base_own": lambda name: project(tp, gate(name, hidden_input), query_weight),
        "base_other": swap(lambda: need("given")),
        "down_pair": send(pair, lambda: down_own),
        "down_near": send(across, lambda: down_own),
        "down_far": send(across, lambda: need("down_pair")),
        "down_out": send(outward, lambda: need("down_near")[:cut]),
        "up_pair": send(pair, lambda: up_own),
        "up_near": send(across, lambda: up_own),
        "up_far": send(across, lambda: need("up_pair")),
        "up_near_out": send(outward, lambda: need("up_near")),
        "up_far_out": send(outward, lambda: need("up_far")),
        "joined": lambda name: join([gate(name, need("away")[0]), *rows_away()[1:]]),
        "moved": send(inward, lambda: need("joined")),
        "low_home": lower_home,
        "low_home_swap": swap(lambda: need("low_home")),
        "rows_home": lift_home,
        "low_away": lower_away,
        "low_away_swap": swap(lambda: need("low_away")),
        "low_sum": sum_away,
        "low_out": send(outward, lambda: need("low_sum")[need("low_sum").shape[0] // 2 :]),
        "rows_away": lift_away,
        "part": finish_home,
        "queries": finish_away,
        "onehots": lambda name: (back_away, back_home),
    }
    for d in (1, 2, 3):
        for side in ("away", "home"):
            steps[f"{side}{d}"] = send(turn[d], lambda d=d, side=side: need(side)[d])
            steps[f"lift_{side}{d}"] = send(turn[d], lambda d=d, side=side: need(f"rows_{side}")[d])
    return need("queries")


def by_gather(hidden_input, query_weight, slot_down_weight, slot_up_weight, request_adapter, adapter_slot):
    local_width = hidden_input.shape[1]
    output_width = slot_up_weight.shape[2]
    total = slot_down_weight.shape[0] * lax.axis_size("rep")
    base_sum = lax.psum_scatter(
        lax.dot_general(
            query_weight, hidden_input, (((0,), (1,)), ((), ())), preferred_element_type=jnp.float32
        ).astype(jnp.bfloat16),
        "tp",
        scatter_dimension=0,
        tiled=True,
    ).astype(jnp.float32)
    slots, position = places(request_adapter, adapter_slot, total)
    target = slots * MOST + position
    buffer = jnp.zeros((total * MOST, local_width), jnp.bfloat16).at[target].set(hidden_input)
    slot_rows = buffer.reshape(total, MOST, local_width)
    lowered = jnp.einsum(
        "amd,adr->amr",
        slot_rows,
        lax.all_gather(slot_down_weight, "rep", axis=0, tiled=True),
        preferred_element_type=jnp.float32,
    )
    lowered = lax.psum(lowered.astype(jnp.bfloat16), "tp")
    lifted = jnp.einsum(
        "amr,are->ame",
        lowered,
        lax.all_gather(slot_up_weight, "rep", axis=0, tiled=True),
        preferred_element_type=jnp.float32,
    )
    lift_rows = lifted.astype(jnp.bfloat16).reshape(total * MOST, output_width)[target]
    return (base_sum.T + lift_rows.astype(jnp.float32)).astype(jnp.bfloat16)


def solution(mesh):
    in_specs = (
        P("rep", "tp"),
        P("tp", None),
        P("rep", "tp", None),
        P("rep", None, "tp"),
        P("rep", None),
        P(),
    )
    out_specs = P("rep", "tp")
    planes = mesh.shape["rep"] == COLUMNS * PLANES and mesh.shape["tp"] == 2
    shards = by_planes if planes else by_gather
    return jax.shard_map(shards, mesh=mesh, in_specs=in_specs, out_specs=out_specs, check_vma=False)
```

```python
import functools

import jax
import jax.numpy as jnp
from jax import lax
from jax.experimental import pallas as pl
from jax.experimental.pallas import tpu as pltpu
from jax.sharding import PartitionSpec as P

MOST = 16
COLUMNS = 4
PLANES = 4
SWAP = [(0, 1), (1, 0)]
LIMIT = 56 * 1024 * 1024
NT = (((1,), (1,)), ((), ()))
TILE = 256


def params(steps=1):
    return pltpu.CompilerParams(dimension_semantics=("arbitrary",) * steps, vmem_limit_bytes=LIMIT)


def cost(flops, size):
    return pl.CostEstimate(flops=flops, bytes_accessed=size, transcendentals=0)


def pack_kernel(target_ref, x_ref, *rest):
    outs, onehot = rest[:-1], rest[-1]

    @pl.when(pl.program_id(0) == 0)
    def _():
        place = lax.broadcasted_iota(jnp.int32, onehot.shape, 0)
        onehot[...] = (place == target_ref[...]).astype(jnp.bfloat16)

    packed = jnp.dot(onehot[...], x_ref[...], preferred_element_type=jnp.float32).astype(jnp.bfloat16)
    at = 0
    for out in outs:
        out[...] = packed[at : at + out.shape[0]]
        at += out.shape[0]


def pack(target, x, parts):
    rows, width = x.shape
    tile = 1024
    return pl.pallas_call(
        pack_kernel,
        grid=(width // tile,),
        in_specs=[pl.BlockSpec((1, rows), lambda i: (0, 0)), pl.BlockSpec((rows, tile), lambda i: (0, i))],
        out_specs=[pl.BlockSpec((part, tile), lambda i: (0, i)) for part in parts],
        out_shape=[jax.ShapeDtypeStruct((part, width), x.dtype) for part in parts],
        scratch_shapes=[pltpu.VMEM((sum(parts), rows), jnp.bfloat16)],
        compiler_params=params(),
        cost_estimate=cost(2 * sum(parts) * rows * width, 2 * (rows + sum(parts)) * width),
        name="pack_rows",
    )(target, x)


def project_kernel(place_ref, x_ref, w_ref, o_ref):
    o_ref[...] = jnp.dot(x_ref[...], w_ref[...], preferred_element_type=jnp.float32).astype(o_ref.dtype)


def project(half, x, w, first, count):
    rows, width = x.shape
    tile = TILE
    steps = w.shape[1] // 2 // tile
    columns = count * tile
    return pl.pallas_call(
        project_kernel,
        grid_spec=pltpu.PrefetchScalarGridSpec(
            num_scalar_prefetch=1,
            grid=(count,),
            in_specs=[
                pl.BlockSpec((rows, width), lambda i, place: (0, 0)),
                pl.BlockSpec((width, tile), lambda i, place: (0, place[0] * steps + first + i)),
            ],
            out_specs=pl.BlockSpec((rows, tile), lambda i, place: (0, i)),
        ),
        out_shape=jax.ShapeDtypeStruct((rows, columns), jnp.bfloat16),
        compiler_params=params(),
        cost_estimate=cost(2 * rows * width * columns, 2 * (rows * width + columns * width + rows * columns)),
        name="project_half",
    )(half.reshape(1), x, w)


def factor_specs(groups, rank, tile):
    specs = []
    for arrays, first, count in groups:
        shape = (count, rank, tile)
        specs += [pl.BlockSpec(shape, lambda k, at=first // count: (at, 0, k))] * len(arrays)
    return specs


def factors(refs, groups):
    at = start = 0
    for held, count in groups:
        total = functools.reduce(jnp.add, [ref[...] for ref in refs[at : at + held]])
        yield start, count, total.reshape(count * total.shape[1], total.shape[2])
        at += held
        start += count


def flat(groups):
    return [array for arrays, _, _ in groups for array in arrays]


def shape_of(groups):
    return [(len(arrays), count) for arrays, _, count in groups]


def down_kernel(groups, sources, *refs):
    xs, ws, o_ref = refs[:sources], refs[sources:-1], refs[-1]
    step = pl.program_id(0)
    sides = sources // COLUMNS
    side_rows = o_ref.shape[0] // sides

    @pl.when(step == 0)
    def _():
        o_ref[...] = jnp.zeros_like(o_ref)

    for start, count, w in factors(ws, groups):
        rank = w.shape[0] // count
        rows = jnp.concatenate([x[start * MOST : (start + count) * MOST] for x in xs], axis=0)
        y = lax.dot_general(rows, w, NT, preferred_element_type=jnp.float32)
        owner = lax.broadcasted_iota(jnp.int32, y.shape, 0) // MOST % count
        y = jnp.where(owner == lax.broadcasted_iota(jnp.int32, y.shape, 1) // rank, y, 0.0)
        part = COLUMNS * count * MOST
        for side in range(sides):
            at = side * side_rows + start * COLUMNS * MOST
            o_ref[at : at + part, : w.shape[0]] += y[side * part : (side + 1) * part]


def down(xs, groups):
    served = sum(count for _, _, count in groups)
    _, rank, width = groups[0][0][0].shape
    tile = 1024
    rows = len(xs) * served * MOST
    wide = max(count for _, _, count in groups) * rank

    def block(section):
        return pl.BlockSpec((served * MOST, tile), lambda k: (section, k))

    return pl.pallas_call(
        functools.partial(down_kernel, shape_of(groups), len(xs)),
        grid=(width // tile,),
        in_specs=[block(section) for _, section in xs] + factor_specs(groups, rank, tile),
        out_specs=pl.BlockSpec((rows, wide), lambda k: (0, 0)),
        out_shape=jax.ShapeDtypeStruct((rows, wide), jnp.float32),
        compiler_params=params(),
        cost_estimate=cost(2 * rows * wide * width, 2 * width * (served * rank + rows)),
        name="down_rows",
    )(*[x for x, _ in xs], *flat(groups))


def lift_kernel(groups, count_y, *refs):
    outs, y = refs[-1 - COLUMNS : -1], refs[-1]
    ys, us = refs[:count_y], refs[count_y : -1 - COLUMNS]

    @pl.when(pl.program_id(0) == 0)
    def _():
        y[...] = functools.reduce(jnp.add, [ref[...] for ref in ys]).astype(jnp.bfloat16)

    for start, count, u in factors(us, groups):
        part = count * MOST
        at = start * COLUMNS * MOST
        low = y[at : at + COLUMNS * part, : u.shape[0]]
        rows = jnp.dot(low, u, preferred_element_type=jnp.float32).astype(jnp.bfloat16)
        for k, out in enumerate(outs):
            out[start * MOST : start * MOST + part] = rows[k * part : (k + 1) * part]


def lift(ys, groups):
    served = sum(count for _, _, count in groups)
    _, rank, columns = groups[0][0][0].shape
    tile = 512
    rows, wide = served * COLUMNS * MOST, ys[0].shape[1]
    return pl.pallas_call(
        functools.partial(lift_kernel, shape_of(groups), len(ys)),
        grid=(columns // tile,),
        in_specs=[pl.BlockSpec((rows, wide), lambda k: (0, 0))] * len(ys) + factor_specs(groups, rank, tile),
        out_specs=[pl.BlockSpec((served * MOST, tile), lambda k: (0, k))] * COLUMNS,
        out_shape=[jax.ShapeDtypeStruct((served * MOST, columns), jnp.bfloat16)] * COLUMNS,
        scratch_shapes=[pltpu.VMEM((rows, wide), jnp.bfloat16)],
        compiler_params=params(),
        cost_estimate=cost(2 * rows * wide * columns, 2 * columns * (served * rank + rows)),
        name="lift_rows",
    )(*ys, *flat(groups))


def finish_kernel(starts, onehot_ref, *rest):
    count = sum(len(own) for own in starts)
    bases, pieces, o_ref = rest[:count], rest[count:-1], rest[-1]
    step = pl.program_id(0)
    lifted = jnp.concatenate([piece[...] for piece in pieces], axis=0)
    total = jnp.dot(onehot_ref[...], lifted, preferred_element_type=jnp.float32)
    at = 0
    for own in starts:
        base = bases[at][...]
        for k in range(1, len(own)):
            base = jnp.where(step >= own[k], bases[at + k][...], base)
        total += base.astype(jnp.float32)
        at += len(own)
    o_ref[...] = total.astype(o_ref.dtype)


def finish(onehot, bases, pieces, tile, dtype):
    rows, columns = onehot.shape[0], pieces[0].shape[1]
    held = onehot.shape[1]
    starts, specs = [], []
    for arrays in bases:
        at, own = 0, []
        for array in arrays:
            steps = array.shape[1] // tile
            own.append(at)
            specs.append(pl.BlockSpec((rows, tile), lambda i, at=at, steps=steps: (0, jnp.clip(i - at, 0, steps - 1))))
            at += steps
        starts.append(own)
    return pl.pallas_call(
        functools.partial(finish_kernel, starts),
        grid=(columns // tile,),
        in_specs=[pl.BlockSpec((rows, held), lambda i: (0, 0)), *specs]
        + [pl.BlockSpec((piece.shape[0], tile), lambda i: (0, i)) for piece in pieces],
        out_specs=pl.BlockSpec((rows, tile), lambda i: (0, i)),
        out_shape=jax.ShapeDtypeStruct((rows, columns), dtype),
        compiler_params=params(),
        cost_estimate=cost(2 * rows * held * columns, 8 * rows * columns),
        name="finish_rows",
    )(onehot, *[array for arrays in bases for array in arrays], *pieces)


def join_kernel(*refs):
    pieces, o_ref = refs[:-1], refs[-1]
    rows = pieces[0].shape[0]
    for k, piece in enumerate(pieces):
        o_ref[k * rows : (k + 1) * rows] = piece[...]


def join(pieces):
    rows, width = pieces[0].shape
    tile = 1024
    return pl.pallas_call(
        join_kernel,
        grid=(width // tile,),
        in_specs=[pl.BlockSpec((rows, tile), lambda k: (0, k))] * len(pieces),
        out_specs=pl.BlockSpec((rows * len(pieces), tile), lambda k: (0, k)),
        out_shape=jax.ShapeDtypeStruct((rows * len(pieces), width), pieces[0].dtype),
        compiler_params=params(),
        cost_estimate=cost(0, 4 * rows * len(pieces) * width),
        name="join_rows",
    )(*pieces)


def places(request_adapter, adapter_slot, total):
    rows = request_adapter.shape[0]
    ids = request_adapter[:, 0]
    names = lax.broadcasted_iota(jnp.int32, (rows, total), 1)
    slots = jnp.sum(jnp.where(ids[:, None] == names, adapter_slot[None, :], 0), axis=1)
    onehot = (slots[:, None] == names).astype(jnp.bfloat16)
    row_iota = lax.broadcasted_iota(jnp.int32, (rows, rows), 0)
    col_iota = lax.broadcasted_iota(jnp.int32, (rows, rows), 1)
    earlier = (row_iota > col_iota).astype(jnp.bfloat16)
    counts = jnp.dot(earlier, onehot, preferred_element_type=jnp.float32)
    position = jnp.sum(counts * onehot.astype(jnp.float32), axis=1).astype(jnp.int32)
    return slots, position


def after(x, *earlier):
    return lax.optimization_barrier((x, *earlier))[0]


def by_planes(hidden_input, query_weight, slot_down_weight, slot_up_weight, request_adapter, adapter_slot):
    owned = slot_down_weight.shape[0]
    cut = owned // 2
    served = 2 * owned + cut
    rest = 4 * owned - served
    me = lax.axis_index("rep")
    plane, column = me // COLUMNS, me % COLUMNS
    every = range(COLUMNS * PLANES)
    inside = [r for r in every if r // COLUMNS in (1, 2)]
    outside = [r for r in every if r // COLUMNS in (0, 3)]

    def send(x, pairs, *earlier):
        return lax.ppermute(after(x, *earlier) if earlier else x, "rep", pairs)

    pair = [(r, r ^ 4) for r in every]
    across = [(r, r ^ 12) for r in inside]
    outward = [(r, r ^ 4) for r in inside]
    inward = [(r, r ^ 4) for r in outside]
    turn = [[(r, r ^ d) for r in every] for d in range(COLUMNS)]

    slots, position = places(request_adapter, adapter_slot, owned * COLUMNS * PLANES)
    slot_plane = slots // (owned * COLUMNS)
    slot_column = slots // owned % COLUMNS
    other = slot_plane // 2 != plane // 2
    second = jnp.where(other, (slot_plane == 0) | (slot_plane == 3), slot_plane != plane)
    number = (2 * other.astype(jnp.int32) + second.astype(jnp.int32)) * owned + slots % owned
    turned = slot_column ^ column
    there = (turned * rest + number - served) * MOST
    here = (COLUMNS * rest + turned * served + number) * MOST
    target = jnp.where(number < served, here, there) + position

    down_own = jnp.swapaxes(slot_down_weight, 1, 2)
    up_own = slot_up_weight
    tp = lax.axis_index("tp")
    tiles = query_weight.shape[1] // 2 // TILE
    early = tiles * 5 // 8
    down_pair = send(down_own, pair)
    down_near = send(down_own, across)

    packed = pack(target[None, :], hidden_input, [rest * MOST] * COLUMNS + [served * MOST] * COLUMNS)
    away, home = packed[:COLUMNS], packed[COLUMNS:]
    away = [away[0]] + [send(away[d], turn[d]) for d in range(1, COLUMNS)]
    given = project(1 - tp, after(hidden_input, home[0]), query_weight, 0, tiles)

    up_pair = send(up_own, pair, down_pair, given)
    up_near = send(up_own, across, down_near, given)
    beside = [home[0]] + [send(home[d], turn[d], away[d], given) for d in (1, 2)]
    moving = join(away)
    base_own = [project(tp, after(hidden_input, down_pair, down_near, moving), query_weight, 0, early)]

    moved = send(moving, inward, up_pair, base_own[0])
    down_out = send(down_near[:cut], outward, up_pair, base_own[0])
    up_far = send(up_pair, across, up_near, base_own[0])
    beside.append(send(home[3], turn[3], beside[1], beside[2], base_own[0]))
    base_own.append(project(tp, after(hidden_input, beside[1], beside[2], up_near), query_weight, early, tiles - early))
    down_far = send(down_pair, across, up_far, down_out)
    up_near_out = send(up_near, outward, down_out, base_own[1])

    split = COLUMNS * rest * MOST
    spots = lax.broadcasted_iota(jnp.int32, (target.shape[0], 4 * owned * COLUMNS * MOST), 1)
    onehot = (after(target, given)[:, None] == spots).astype(jnp.bfloat16)
    back_away, back_home = onehot[:, :split], onehot[:, split:]

    def swapped(y, *earlier):
        return lax.ppermute(after(y, *earlier) if earlier else y, "tp", SWAP)

    low = down(
        [(after(beside[0], base_own[1]), 0)] + [(rows, 0) for rows in beside[1:]],
        [([down_own], 0, owned), ([down_pair], 0, owned), ([down_near, down_out], 0, cut)],
    )
    up_far_out = send(up_far, outward, up_near_out, low)
    rows = lift(
        [low, swapped(low)], [([up_own], 0, owned), ([up_pair], 0, owned), ([up_near, up_near_out], 0, cut)]
    )
    lifted_home = [rows[0]] + [send(rows[d], turn[d]) for d in (1, 2)]
    lifted_home.append(send(rows[3], turn[3], lifted_home[1]))

    low = down(
        [(after(away[0], up_far_out, lifted_home[1], lifted_home[2]), 0)]
        + [(rows, 0) for rows in away[1:]]
        + [(moved, d) for d in range(COLUMNS)],
        [([down_near], cut, owned - cut), ([down_far], 0, owned)],
    )
    low_other = swapped(low)
    base_other = swapped(given, low_other)
    low = (low + low_other).astype(jnp.bfloat16)
    rows = lift(
        [low, send(low[low.shape[0] // 2 :], outward)],
        [([up_near, up_near_out], cut, owned - cut), ([up_far, up_far_out], 0, owned)],
    )
    lifted_away = [rows[0]] + [send(rows[d], turn[d]) for d in range(1, COLUMNS)]
    base_own[0] = after(base_own[0], rows[0])
    part = finish(back_home, [base_own, [base_other]], lifted_home, TILE, jnp.float32)
    return finish(back_away, [[part]], lifted_away, 2 * TILE, jnp.bfloat16)


def by_gather(hidden_input, query_weight, slot_down_weight, slot_up_weight, request_adapter, adapter_slot):
    local_width = hidden_input.shape[1]
    output_width = slot_up_weight.shape[2]
    total = slot_down_weight.shape[0] * lax.axis_size("rep")
    base_sum = lax.psum_scatter(
        lax.dot_general(
            query_weight, hidden_input, (((0,), (1,)), ((), ())), preferred_element_type=jnp.float32
        ).astype(jnp.bfloat16),
        "tp",
        scatter_dimension=0,
        tiled=True,
    ).astype(jnp.float32)
    slots, position = places(request_adapter, adapter_slot, total)
    target = slots * MOST + position
    buffer = jnp.zeros((total * MOST, local_width), jnp.bfloat16).at[target].set(hidden_input)
    slot_rows = buffer.reshape(total, MOST, local_width)
    lowered = jnp.einsum(
        "amd,adr->amr",
        slot_rows,
        lax.all_gather(slot_down_weight, "rep", axis=0, tiled=True),
        preferred_element_type=jnp.float32,
    )
    lowered = lax.psum(lowered.astype(jnp.bfloat16), "tp")
    lifted = jnp.einsum(
        "amr,are->ame",
        lowered,
        lax.all_gather(slot_up_weight, "rep", axis=0, tiled=True),
        preferred_element_type=jnp.float32,
    )
    lift_rows = lifted.astype(jnp.bfloat16).reshape(total * MOST, output_width)[target]
    return (base_sum.T + lift_rows.astype(jnp.float32)).astype(jnp.bfloat16)


def solution(mesh):
    in_specs = (
        P("rep", "tp"),
        P("tp", None),
        P("rep", "tp", None),
        P("rep", None, "tp"),
        P("rep", None),
        P(),
    )
    out_specs = P("rep", "tp")
    planes = mesh.shape["rep"] == COLUMNS * PLANES and mesh.shape["tp"] == 2
    shards = by_planes if planes else by_gather
    return jax.shard_map(shards, mesh=mesh, in_specs=in_specs, out_specs=out_specs, check_vma=False)
```

```python
import functools

import jax
import jax.numpy as jnp
from jax import lax
from jax.experimental import pallas as pl
from jax.experimental.pallas import tpu as pltpu
from jax.sharding import PartitionSpec as P

MOST = 16
COLUMNS = 4
PLANES = 4
SWAP = [(0, 1), (1, 0)]
LIMIT = 63 * 1024 * 1024
NT = (((1,), (1,)), ((), ()))
TILE = 256


def params(steps=1):
    return pltpu.CompilerParams(dimension_semantics=("arbitrary",) * steps, vmem_limit_bytes=LIMIT)


def cost(flops, size):
    return pl.CostEstimate(flops=flops, bytes_accessed=size, transcendentals=0)


def pack_kernel(target_ref, x_ref, *rest):
    outs, onehot = rest[:-1], rest[-1]

    @pl.when(pl.program_id(0) == 0)
    def _():
        place = lax.broadcasted_iota(jnp.int32, onehot.shape, 0)
        onehot[...] = (place == target_ref[...]).astype(jnp.bfloat16)

    packed = jnp.dot(onehot[...], x_ref[...], preferred_element_type=jnp.float32).astype(jnp.bfloat16)
    at = 0
    for out in outs:
        out[...] = packed[at : at + out.shape[0]]
        at += out.shape[0]


def pack(target, x, parts):
    rows, width = x.shape
    tile = 1024
    return pl.pallas_call(
        pack_kernel,
        grid=(width // tile,),
        in_specs=[pl.BlockSpec((1, rows), lambda i: (0, 0)), pl.BlockSpec((rows, tile), lambda i: (0, i))],
        out_specs=[pl.BlockSpec((part, tile), lambda i: (0, i)) for part in parts],
        out_shape=[jax.ShapeDtypeStruct((part, width), x.dtype) for part in parts],
        scratch_shapes=[pltpu.VMEM((sum(parts), rows), jnp.bfloat16)],
        compiler_params=params(),
        cost_estimate=cost(2 * sum(parts) * rows * width, 2 * (rows + sum(parts)) * width),
        name="pack_rows",
    )(target, x)


def project_kernel(counts, place_ref, x_ref, w_ref, *outs):
    step, at = pl.program_id(0), 0
    product = jnp.dot(x_ref[...], w_ref[...], preferred_element_type=jnp.float32).astype(jnp.bfloat16)
    for out, count in zip(outs, counts):

        @pl.when((step >= at) & (step < at + count))
        def _():
            out[...] = product

        at += count


def project(tp, x, w, parts):
    rows, width = x.shape
    tile = TILE
    steps = w.shape[1] // 2 // tile
    counts = [count for _, _, count in parts]
    firsts = jnp.stack([(1 - tp if given else tp) * steps + first for given, first, _ in parts])
    columns = sum(counts) * tile

    def w_tile(i, place):
        at, found = 0, place[0] + i
        for k, count in enumerate(counts):
            found = jnp.where(i >= at, place[k] + i - at, found)
            at += count
        return 0, found

    def out_spec(at, count):
        return pl.BlockSpec((rows, tile), lambda i, place: (0, jnp.clip(i - at, 0, count - 1)))

    return pl.pallas_call(
        functools.partial(project_kernel, counts),
        grid_spec=pltpu.PrefetchScalarGridSpec(
            num_scalar_prefetch=1,
            grid=(sum(counts),),
            in_specs=[
                pl.BlockSpec((rows, width), lambda i, place: (0, 0)),
                pl.BlockSpec((width, tile), w_tile),
            ],
            out_specs=[out_spec(sum(counts[:k]), count) for k, count in enumerate(counts)],
        ),
        out_shape=[jax.ShapeDtypeStruct((rows, count * tile), jnp.bfloat16) for count in counts],
        compiler_params=params(),
        cost_estimate=cost(2 * rows * width * columns, 2 * (rows * width + columns * width + rows * columns)),
        name="project_half",
    )(firsts, x, w)


def factor_specs(groups, rank, tile):
    specs = []
    for arrays, first, count in groups:
        shape = (count, rank, tile)
        specs += [pl.BlockSpec(shape, lambda k, at=first // count: (at, 0, k))] * len(arrays)
    return specs


def factors(refs, groups):
    at = start = 0
    for held, count in groups:
        total = functools.reduce(jnp.add, [ref[...] for ref in refs[at : at + held]])
        yield start, count, total.reshape(count * total.shape[1], total.shape[2])
        at += held
        start += count


def flat(groups):
    return [array for arrays, _, _ in groups for array in arrays]


def shape_of(groups):
    return [(len(arrays), count) for arrays, _, count in groups]


def down_kernel(groups, sources, *refs):
    xs, ws, o_ref = refs[:sources], refs[sources:-1], refs[-1]
    step = pl.program_id(0)
    sides = sources // COLUMNS
    side_rows = o_ref.shape[0] // sides

    @pl.when(step == 0)
    def _():
        o_ref[...] = jnp.zeros_like(o_ref)

    for start, count, w in factors(ws, groups):
        rank = w.shape[0] // count
        rows = jnp.concatenate([x[start * MOST : (start + count) * MOST] for x in xs], axis=0)
        y = lax.dot_general(rows, w, NT, preferred_element_type=jnp.float32)
        owner = lax.broadcasted_iota(jnp.int32, y.shape, 0) // MOST % count
        y = jnp.where(owner == lax.broadcasted_iota(jnp.int32, y.shape, 1) // rank, y, 0.0)
        part = COLUMNS * count * MOST
        for side in range(sides):
            at = side * side_rows + start * COLUMNS * MOST
            o_ref[at : at + part, : w.shape[0]] += y[side * part : (side + 1) * part]


def down(xs, groups):
    served = sum(count for _, _, count in groups)
    _, rank, width = groups[0][0][0].shape
    tile = 1024
    rows = len(xs) * served * MOST
    wide = max(count for _, _, count in groups) * rank

    def block(section):
        return pl.BlockSpec((served * MOST, tile), lambda k: (section, k))

    return pl.pallas_call(
        functools.partial(down_kernel, shape_of(groups), len(xs)),
        grid=(width // tile,),
        in_specs=[block(section) for _, section in xs] + factor_specs(groups, rank, tile),
        out_specs=pl.BlockSpec((rows, wide), lambda k: (0, 0)),
        out_shape=jax.ShapeDtypeStruct((rows, wide), jnp.float32),
        compiler_params=params(),
        cost_estimate=cost(2 * rows * wide * width, 2 * width * (served * rank + rows)),
        name="down_rows",
    )(*[x for x, _ in xs], *flat(groups))


def lift_kernel(groups, count_y, *refs):
    outs, y = refs[-1 - COLUMNS : -1], refs[-1]
    ys, us = refs[:count_y], refs[count_y : -1 - COLUMNS]

    @pl.when(pl.program_id(0) == 0)
    def _():
        y[...] = functools.reduce(jnp.add, [ref[...] for ref in ys]).astype(jnp.bfloat16)

    for start, count, u in factors(us, groups):
        part = count * MOST
        at = start * COLUMNS * MOST
        low = y[at : at + COLUMNS * part, : u.shape[0]]
        rows = jnp.dot(low, u, preferred_element_type=jnp.float32).astype(jnp.bfloat16)
        for k, out in enumerate(outs):
            out[start * MOST : start * MOST + part] = rows[k * part : (k + 1) * part]


def lift(ys, groups):
    served = sum(count for _, _, count in groups)
    _, rank, columns = groups[0][0][0].shape
    tile = 512
    rows, wide = served * COLUMNS * MOST, ys[0].shape[1]
    return pl.pallas_call(
        functools.partial(lift_kernel, shape_of(groups), len(ys)),
        grid=(columns // tile,),
        in_specs=[pl.BlockSpec((rows, wide), lambda k: (0, 0))] * len(ys) + factor_specs(groups, rank, tile),
        out_specs=[pl.BlockSpec((served * MOST, tile), lambda k: (0, k))] * COLUMNS,
        out_shape=[jax.ShapeDtypeStruct((served * MOST, columns), jnp.bfloat16)] * COLUMNS,
        scratch_shapes=[pltpu.VMEM((rows, wide), jnp.bfloat16)],
        compiler_params=params(),
        cost_estimate=cost(2 * rows * wide * columns, 2 * columns * (served * rank + rows)),
        name="lift_rows",
    )(*ys, *flat(groups))


def finish_kernel(starts, onehot_ref, *rest):
    count = sum(len(own) for own in starts)
    bases, pieces, o_ref = rest[:count], rest[count:-1], rest[-1]
    step = pl.program_id(0)
    lifted = jnp.concatenate([piece[...] for piece in pieces], axis=0)
    total = jnp.dot(onehot_ref[...], lifted, preferred_element_type=jnp.float32)
    at = 0
    for own in starts:
        base = bases[at][...]
        for k in range(1, len(own)):
            base = jnp.where(step >= own[k], bases[at + k][...], base)
        total += base.astype(jnp.float32)
        at += len(own)
    o_ref[...] = total.astype(o_ref.dtype)


def finish(onehot, bases, pieces, tile, dtype):
    rows, columns = onehot.shape[0], pieces[0].shape[1]
    held = onehot.shape[1]
    starts, specs = [], []
    for arrays in bases:
        at, own = 0, []
        for array in arrays:
            steps = array.shape[1] // tile
            own.append(at)
            specs.append(pl.BlockSpec((rows, tile), lambda i, at=at, steps=steps: (0, jnp.clip(i - at, 0, steps - 1))))
            at += steps
        starts.append(own)
    return pl.pallas_call(
        functools.partial(finish_kernel, starts),
        grid=(columns // tile,),
        in_specs=[pl.BlockSpec((rows, held), lambda i: (0, 0)), *specs]
        + [pl.BlockSpec((piece.shape[0], tile), lambda i: (0, i)) for piece in pieces],
        out_specs=pl.BlockSpec((rows, tile), lambda i: (0, i)),
        out_shape=jax.ShapeDtypeStruct((rows, columns), dtype),
        compiler_params=params(),
        cost_estimate=cost(2 * rows * held * columns, 8 * rows * columns),
        name="finish_rows",
    )(onehot, *[array for arrays in bases for array in arrays], *pieces)


def join_kernel(*refs):
    pieces, o_ref = refs[:-1], refs[-1]
    rows = pieces[0].shape[0]
    for k, piece in enumerate(pieces):
        o_ref[k * rows : (k + 1) * rows] = piece[...]


def join(pieces):
    rows, width = pieces[0].shape
    tile = 1024
    return pl.pallas_call(
        join_kernel,
        grid=(width // tile,),
        in_specs=[pl.BlockSpec((rows, tile), lambda k: (0, k))] * len(pieces),
        out_specs=pl.BlockSpec((rows * len(pieces), tile), lambda k: (0, k)),
        out_shape=jax.ShapeDtypeStruct((rows * len(pieces), width), pieces[0].dtype),
        compiler_params=params(),
        cost_estimate=cost(0, 4 * rows * len(pieces) * width),
        name="join_rows",
    )(*pieces)


def places(request_adapter, adapter_slot, total):
    rows = request_adapter.shape[0]
    ids = request_adapter[:, 0]
    names = lax.broadcasted_iota(jnp.int32, (rows, total), 1)
    slots = jnp.sum(jnp.where(ids[:, None] == names, adapter_slot[None, :], 0), axis=1)
    onehot = (slots[:, None] == names).astype(jnp.bfloat16)
    row_iota = lax.broadcasted_iota(jnp.int32, (rows, rows), 0)
    col_iota = lax.broadcasted_iota(jnp.int32, (rows, rows), 1)
    earlier = (row_iota > col_iota).astype(jnp.bfloat16)
    counts = jnp.dot(earlier, onehot, preferred_element_type=jnp.float32)
    position = jnp.sum(counts * onehot.astype(jnp.float32), axis=1).astype(jnp.int32)
    return slots, position


def after(x, *earlier):
    return lax.optimization_barrier((x, *earlier))[0]


def by_planes(hidden_input, query_weight, slot_down_weight, slot_up_weight, request_adapter, adapter_slot):
    owned = slot_down_weight.shape[0]
    cut = owned // 2
    served = 2 * owned + cut
    rest = 4 * owned - served
    me = lax.axis_index("rep")
    plane, column = me // COLUMNS, me % COLUMNS
    every = range(COLUMNS * PLANES)
    inside = [r for r in every if r // COLUMNS in (1, 2)]
    outside = [r for r in every if r // COLUMNS in (0, 3)]

    def send(x, pairs, *earlier):
        return lax.ppermute(after(x, *earlier) if earlier else x, "rep", pairs)

    pair = [(r, r ^ 4) for r in every]
    across = [(r, r ^ 12) for r in inside]
    outward = [(r, r ^ 4) for r in inside]
    inward = [(r, r ^ 4) for r in outside]
    turn = [[(r, r ^ d) for r in every] for d in range(COLUMNS)]

    slots, position = places(request_adapter, adapter_slot, owned * COLUMNS * PLANES)
    slot_plane = slots // (owned * COLUMNS)
    slot_column = slots // owned % COLUMNS
    other = slot_plane // 2 != plane // 2
    second = jnp.where(other, (slot_plane == 0) | (slot_plane == 3), slot_plane != plane)
    number = (2 * other.astype(jnp.int32) + second.astype(jnp.int32)) * owned + slots % owned
    turned = slot_column ^ column
    there = (turned * rest + number - served) * MOST
    here = (COLUMNS * rest + turned * served + number) * MOST
    target = jnp.where(number < served, here, there) + position

    down_own = jnp.swapaxes(slot_down_weight, 1, 2)
    up_own = slot_up_weight
    tp = lax.axis_index("tp")
    tiles = query_weight.shape[1] // 2 // TILE
    first, second = tiles // 4, tiles * 5 // 8
    down_pair = send(down_own, pair)
    down_near = send(down_own, across)

    packed = pack(target[None, :], hidden_input, [rest * MOST] * COLUMNS + [served * MOST] * COLUMNS)
    away, home = packed[:COLUMNS], packed[COLUMNS:]
    away = [away[0]] + [send(away[d], turn[d]) for d in range(1, COLUMNS)]
    given, own = project(tp, after(hidden_input, home[0]), query_weight, [(True, 0, tiles), (False, 0, first)])
    base_own = [own]

    up_pair = send(up_own, pair, down_pair, given)
    up_near = send(up_own, across, down_near, given)
    beside = [home[0]] + [send(home[d], turn[d], away[d], given) for d in (1, 2)]
    moving = join(away)
    base_own += project(tp, after(hidden_input, down_pair, down_near, moving), query_weight, [(False, first, second - first)])

    moved = send(moving, inward, up_pair, base_own[1])
    down_out = send(down_near[:cut], outward, up_pair, base_own[1])
    up_far = send(up_pair, across, up_near, base_own[1])
    beside.append(send(home[3], turn[3], beside[1], beside[2], base_own[1]))
    late = after(hidden_input, beside[1], beside[2], up_near)
    base_own += project(tp, late, query_weight, [(False, second, tiles - second)])
    down_far = send(down_pair, across, up_far, down_out)
    up_near_out = send(up_near, outward, down_out, base_own[2])

    split = COLUMNS * rest * MOST
    spots = lax.broadcasted_iota(jnp.int32, (target.shape[0], 4 * owned * COLUMNS * MOST), 1)
    onehot = (after(target, given)[:, None] == spots).astype(jnp.bfloat16)
    back_away, back_home = onehot[:, :split], onehot[:, split:]

    def swapped(y, *earlier):
        return lax.ppermute(after(y, *earlier) if earlier else y, "tp", SWAP)

    low = down(
        [(after(beside[0], base_own[2]), 0)] + [(rows, 0) for rows in beside[1:]],
        [([down_own], 0, owned), ([down_pair], 0, owned), ([down_near, down_out], 0, cut)],
    )
    up_far_out = send(up_far, outward, up_near_out, low)
    rows = lift(
        [low, swapped(low)], [([up_own], 0, owned), ([up_pair], 0, owned), ([up_near, up_near_out], 0, cut)]
    )
    lifted_home = [rows[0]] + [send(rows[d], turn[d]) for d in (1, 2)]
    lifted_home.append(send(rows[3], turn[3], lifted_home[1]))

    low = down(
        [(after(away[0], up_far_out, lifted_home[1], lifted_home[2]), 0)]
        + [(rows, 0) for rows in away[1:]]
        + [(moved, d) for d in range(COLUMNS)],
        [([down_near], cut, owned - cut), ([down_far], 0, owned)],
    )
    low_other = swapped(low)
    base_other = swapped(given, low_other)
    low = (low + low_other).astype(jnp.bfloat16)
    rows = lift(
        [low, send(low[low.shape[0] // 2 :], outward)],
        [([up_near, up_near_out], cut, owned - cut), ([up_far, up_far_out], 0, owned)],
    )
    lifted_away = [rows[0]] + [send(rows[d], turn[d]) for d in range(1, COLUMNS)]
    base_own[0] = after(base_own[0], rows[0])
    part = finish(back_home, [base_own, [base_other]], lifted_home, TILE, jnp.float32)
    return finish(back_away, [[part]], lifted_away, 2 * TILE, jnp.bfloat16)


def by_gather(hidden_input, query_weight, slot_down_weight, slot_up_weight, request_adapter, adapter_slot):
    local_width = hidden_input.shape[1]
    output_width = slot_up_weight.shape[2]
    total = slot_down_weight.shape[0] * lax.axis_size("rep")
    base_sum = lax.psum_scatter(
        lax.dot_general(
            query_weight, hidden_input, (((0,), (1,)), ((), ())), preferred_element_type=jnp.float32
        ).astype(jnp.bfloat16),
        "tp",
        scatter_dimension=0,
        tiled=True,
    ).astype(jnp.float32)
    slots, position = places(request_adapter, adapter_slot, total)
    target = slots * MOST + position
    buffer = jnp.zeros((total * MOST, local_width), jnp.bfloat16).at[target].set(hidden_input)
    slot_rows = buffer.reshape(total, MOST, local_width)
    lowered = jnp.einsum(
        "amd,adr->amr",
        slot_rows,
        lax.all_gather(slot_down_weight, "rep", axis=0, tiled=True),
        preferred_element_type=jnp.float32,
    )
    lowered = lax.psum(lowered.astype(jnp.bfloat16), "tp")
    lifted = jnp.einsum(
        "amr,are->ame",
        lowered,
        lax.all_gather(slot_up_weight, "rep", axis=0, tiled=True),
        preferred_element_type=jnp.float32,
    )
    lift_rows = lifted.astype(jnp.bfloat16).reshape(total * MOST, output_width)[target]
    return (base_sum.T + lift_rows.astype(jnp.float32)).astype(jnp.bfloat16)


def solution(mesh):
    in_specs = (
        P("rep", "tp"),
        P("tp", None),
        P("rep", "tp", None),
        P("rep", None, "tp"),
        P("rep", None),
        P(),
    )
    out_specs = P("rep", "tp")
    planes = mesh.shape["rep"] == COLUMNS * PLANES and mesh.shape["tp"] == 2
    shards = by_planes if planes else by_gather
    return jax.shard_map(shards, mesh=mesh, in_specs=in_specs, out_specs=out_specs, check_vma=False)
```

```python
import functools

import jax
import jax.numpy as jnp
from jax import lax
from jax.experimental import pallas as pl
from jax.experimental.pallas import tpu as pltpu
from jax.sharding import PartitionSpec as P

MOST = 16
COLUMNS = 4
PLANES = 4
SWAP = [(0, 1), (1, 0)]
LIMIT = 63 * 1024 * 1024
NT = (((1,), (1,)), ((), ()))
TILE = 256


def params(steps=1):
    return pltpu.CompilerParams(dimension_semantics=("arbitrary",) * steps, vmem_limit_bytes=LIMIT)


def cost(flops, size):
    return pl.CostEstimate(flops=flops, bytes_accessed=size, transcendentals=0)


def pack_kernel(target_ref, x_ref, *rest):
    outs, onehot = rest[:-1], rest[-1]

    @pl.when(pl.program_id(0) == 0)
    def _():
        place = lax.broadcasted_iota(jnp.int32, onehot.shape, 0)
        onehot[...] = (place == target_ref[...]).astype(jnp.bfloat16)

    packed = jnp.dot(onehot[...], x_ref[...], preferred_element_type=jnp.float32).astype(jnp.bfloat16)
    at = 0
    for out in outs:
        out[...] = packed[at : at + out.shape[0]]
        at += out.shape[0]


def pack(target, x, parts):
    rows, width = x.shape
    tile = 1024
    return pl.pallas_call(
        pack_kernel,
        grid=(width // tile,),
        in_specs=[pl.BlockSpec((1, rows), lambda i: (0, 0)), pl.BlockSpec((rows, tile), lambda i: (0, i))],
        out_specs=[pl.BlockSpec((part, tile), lambda i: (0, i)) for part in parts],
        out_shape=[jax.ShapeDtypeStruct((part, width), x.dtype) for part in parts],
        scratch_shapes=[pltpu.VMEM((sum(parts), rows), jnp.bfloat16)],
        compiler_params=params(),
        cost_estimate=cost(2 * sum(parts) * rows * width, 2 * (rows + sum(parts)) * width),
        name="pack_rows",
    )(target, x)


def project_kernel(counts, place_ref, x_ref, w_ref, *outs):
    step, at = pl.program_id(0), 0
    product = jnp.dot(x_ref[...], w_ref[...], preferred_element_type=jnp.float32).astype(jnp.bfloat16)
    for out, count in zip(outs, counts):

        @pl.when((step >= at) & (step < at + count))
        def _():
            out[...] = product

        at += count


def project(tp, x, w, parts):
    rows, width = x.shape
    tile = TILE
    steps = w.shape[1] // 2 // tile
    counts = [count for _, _, count in parts]
    firsts = jnp.stack([(1 - tp if given else tp) * steps + first for given, first, _ in parts])
    columns = sum(counts) * tile

    def w_tile(i, place):
        at, found = 0, place[0] + i
        for k, count in enumerate(counts):
            found = jnp.where(i >= at, place[k] + i - at, found)
            at += count
        return 0, found

    def out_spec(at, count):
        return pl.BlockSpec((rows, tile), lambda i, place: (0, jnp.clip(i - at, 0, count - 1)))

    return pl.pallas_call(
        functools.partial(project_kernel, counts),
        grid_spec=pltpu.PrefetchScalarGridSpec(
            num_scalar_prefetch=1,
            grid=(sum(counts),),
            in_specs=[
                pl.BlockSpec((rows, width), lambda i, place: (0, 0)),
                pl.BlockSpec((width, tile), w_tile),
            ],
            out_specs=[out_spec(sum(counts[:k]), count) for k, count in enumerate(counts)],
        ),
        out_shape=[jax.ShapeDtypeStruct((rows, count * tile), jnp.bfloat16) for count in counts],
        compiler_params=params(),
        cost_estimate=cost(2 * rows * width * columns, 2 * (rows * width + columns * width + rows * columns)),
        name="project_half",
    )(firsts, x, w)


def factor_specs(groups, rank, tile):
    specs = []
    for arrays, first, count in groups:
        shape = (count, rank, tile)
        specs += [pl.BlockSpec(shape, lambda k, at=first // count: (at, 0, k))] * len(arrays)
    return specs


def factors(refs, groups):
    at = start = 0
    for held, count in groups:
        total = functools.reduce(jnp.add, [ref[...] for ref in refs[at : at + held]])
        yield start, count, total.reshape(count * total.shape[1], total.shape[2])
        at += held
        start += count


def flat(groups):
    return [array for arrays, _, _ in groups for array in arrays]


def shape_of(groups):
    return [(len(arrays), count) for arrays, _, count in groups]


def owned_by(shape, count):
    owner = lax.broadcasted_iota(jnp.int32, shape, 0) // MOST % count
    return owner == lax.broadcasted_iota(jnp.int32, shape, 1) // (shape[1] // count)


def down_kernel(groups, sources, *refs):
    xs, ws, o_ref, total = refs[:sources], refs[sources:-2], refs[-2], refs[-1]
    step = pl.program_id(0)
    rank = o_ref.shape[1]
    sides = sources // COLUMNS
    side_rows = o_ref.shape[0] // sides

    @pl.when(step == 0)
    def _():
        total[...] = jnp.zeros_like(total)

    for start, count, w in factors(ws, groups):
        rows = jnp.concatenate([x[start * MOST : (start + count) * MOST] for x in xs], axis=0)
        at = start * sources * MOST
        total[at : at + rows.shape[0], : w.shape[0]] += lax.dot_general(
            rows, w, NT, preferred_element_type=jnp.float32
        )

    @pl.when(step == pl.num_programs(0) - 1)
    def _():
        start = 0
        for _, count in groups:
            at, part = start * sources * MOST, COLUMNS * count * MOST
            y = total[at : at + sides * part, : count * rank]
            y = jnp.where(owned_by(y.shape, count), y, 0.0)
            y = functools.reduce(jnp.add, [y[:, k * rank : (k + 1) * rank] for k in range(count)])
            for side in range(sides):
                to = side * side_rows + start * COLUMNS * MOST
                o_ref[to : to + part] = y[side * part : (side + 1) * part]
            start += count


def down(xs, groups):
    served = sum(count for _, _, count in groups)
    _, rank, width = groups[0][0][0].shape
    tile = 1024
    rows = len(xs) * served * MOST
    wide = max(count for _, _, count in groups) * rank

    def block(section):
        return pl.BlockSpec((served * MOST, tile), lambda k: (section, k))

    return pl.pallas_call(
        functools.partial(down_kernel, shape_of(groups), len(xs)),
        grid=(width // tile,),
        in_specs=[block(section) for _, section in xs] + factor_specs(groups, rank, tile),
        out_specs=pl.BlockSpec((rows, rank), lambda k: (0, 0)),
        out_shape=jax.ShapeDtypeStruct((rows, rank), jnp.float32),
        scratch_shapes=[pltpu.VMEM((rows, wide), jnp.float32)],
        compiler_params=params(),
        cost_estimate=cost(2 * rows * wide * width, 2 * width * (served * rank + rows)),
        name="down_rows",
    )(*[x for x, _ in xs], *flat(groups))


def lift_kernel(groups, count_y, *refs):
    outs, y = refs[-1 - COLUMNS : -1], refs[-1]
    ys, us = refs[:count_y], refs[count_y : -1 - COLUMNS]

    @pl.when(pl.program_id(0) == 0)
    def _():
        low = functools.reduce(jnp.add, [ref[...] for ref in ys]).astype(jnp.float32)
        at = 0
        for _, count in groups:
            part = COLUMNS * count * MOST
            wide = jnp.concatenate([low[at : at + part]] * count, axis=1)
            wide = jnp.where(owned_by(wide.shape, count), wide, 0.0)
            y[at : at + part, : wide.shape[1]] = wide.astype(jnp.bfloat16)
            at += part

    for start, count, u in factors(us, groups):
        part = count * MOST
        at = start * COLUMNS * MOST
        low = y[at : at + COLUMNS * part, : u.shape[0]]
        rows = jnp.dot(low, u, preferred_element_type=jnp.float32).astype(jnp.bfloat16)
        for k, out in enumerate(outs):
            out[start * MOST : start * MOST + part] = rows[k * part : (k + 1) * part]


def lift(ys, groups):
    served = sum(count for _, _, count in groups)
    _, rank, columns = groups[0][0][0].shape
    tile = 512
    rows, wide = served * COLUMNS * MOST, max(count for _, _, count in groups) * rank
    return pl.pallas_call(
        functools.partial(lift_kernel, shape_of(groups), len(ys)),
        grid=(columns // tile,),
        in_specs=[pl.BlockSpec((rows, rank), lambda k: (0, 0))] * len(ys) + factor_specs(groups, rank, tile),
        out_specs=[pl.BlockSpec((served * MOST, tile), lambda k: (0, k))] * COLUMNS,
        out_shape=[jax.ShapeDtypeStruct((served * MOST, columns), jnp.bfloat16)] * COLUMNS,
        scratch_shapes=[pltpu.VMEM((rows, wide), jnp.bfloat16)],
        compiler_params=params(),
        cost_estimate=cost(2 * rows * wide * columns, 2 * columns * (served * rank + rows)),
        name="lift_rows",
    )(*ys, *flat(groups))


def finish_kernel(starts, onehot_ref, *rest):
    count = sum(len(own) for own in starts)
    bases, pieces, o_ref = rest[:count], rest[count:-1], rest[-1]
    step = pl.program_id(0)
    lifted = jnp.concatenate([piece[...] for piece in pieces], axis=0)
    total = jnp.dot(onehot_ref[...], lifted, preferred_element_type=jnp.float32)
    at = 0
    for own in starts:
        base = bases[at][...]
        for k in range(1, len(own)):
            base = jnp.where(step >= own[k], bases[at + k][...], base)
        total += base.astype(jnp.float32)
        at += len(own)
    o_ref[...] = total.astype(o_ref.dtype)


def finish(onehot, bases, pieces, tile, dtype):
    rows, columns = onehot.shape[0], pieces[0].shape[1]
    held = onehot.shape[1]
    starts, specs = [], []
    for arrays in bases:
        at, own = 0, []
        for array in arrays:
            steps = array.shape[1] // tile
            own.append(at)
            specs.append(pl.BlockSpec((rows, tile), lambda i, at=at, steps=steps: (0, jnp.clip(i - at, 0, steps - 1))))
            at += steps
        starts.append(own)
    return pl.pallas_call(
        functools.partial(finish_kernel, starts),
        grid=(columns // tile,),
        in_specs=[pl.BlockSpec((rows, held), lambda i: (0, 0)), *specs]
        + [pl.BlockSpec((piece.shape[0], tile), lambda i: (0, i)) for piece in pieces],
        out_specs=pl.BlockSpec((rows, tile), lambda i: (0, i)),
        out_shape=jax.ShapeDtypeStruct((rows, columns), dtype),
        compiler_params=params(),
        cost_estimate=cost(2 * rows * held * columns, 8 * rows * columns),
        name="finish_rows",
    )(onehot, *[array for arrays in bases for array in arrays], *pieces)


def join_kernel(*refs):
    pieces, o_ref = refs[:-1], refs[-1]
    rows = pieces[0].shape[0]
    for k, piece in enumerate(pieces):
        o_ref[k * rows : (k + 1) * rows] = piece[...]


def join(pieces):
    rows, width = pieces[0].shape
    tile = 1024
    return pl.pallas_call(
        join_kernel,
        grid=(width // tile,),
        in_specs=[pl.BlockSpec((rows, tile), lambda k: (0, k))] * len(pieces),
        out_specs=pl.BlockSpec((rows * len(pieces), tile), lambda k: (0, k)),
        out_shape=jax.ShapeDtypeStruct((rows * len(pieces), width), pieces[0].dtype),
        compiler_params=params(),
        cost_estimate=cost(0, 4 * rows * len(pieces) * width),
        name="join_rows",
    )(*pieces)


def places(request_adapter, adapter_slot, total):
    rows = request_adapter.shape[0]
    ids = request_adapter[:, 0]
    names = lax.broadcasted_iota(jnp.int32, (rows, total), 1)
    slots = jnp.sum(jnp.where(ids[:, None] == names, adapter_slot[None, :], 0), axis=1)
    onehot = (slots[:, None] == names).astype(jnp.bfloat16)
    row_iota = lax.broadcasted_iota(jnp.int32, (rows, rows), 0)
    col_iota = lax.broadcasted_iota(jnp.int32, (rows, rows), 1)
    earlier = (row_iota > col_iota).astype(jnp.bfloat16)
    counts = jnp.dot(earlier, onehot, preferred_element_type=jnp.float32)
    position = jnp.sum(counts * onehot.astype(jnp.float32), axis=1).astype(jnp.int32)
    return slots, position


def after(x, *earlier):
    return lax.optimization_barrier((x, *earlier))[0]


def by_planes(hidden_input, query_weight, slot_down_weight, slot_up_weight, request_adapter, adapter_slot):
    owned = slot_down_weight.shape[0]
    cut = owned // 2
    served = 2 * owned + cut
    rest = 4 * owned - served
    me = lax.axis_index("rep")
    plane, column = me // COLUMNS, me % COLUMNS
    every = range(COLUMNS * PLANES)
    inside = [r for r in every if r // COLUMNS in (1, 2)]
    outside = [r for r in every if r // COLUMNS in (0, 3)]

    def send(x, pairs, *earlier):
        return lax.ppermute(after(x, *earlier) if earlier else x, "rep", pairs)

    pair = [(r, r ^ 4) for r in every]
    across = [(r, r ^ 12) for r in inside]
    outward = [(r, r ^ 4) for r in inside]
    inward = [(r, r ^ 4) for r in outside]
    turn = [[(r, r ^ d) for r in every] for d in range(COLUMNS)]

    slots, position = places(request_adapter, adapter_slot, owned * COLUMNS * PLANES)
    slot_plane = slots // (owned * COLUMNS)
    slot_column = slots // owned % COLUMNS
    other = slot_plane // 2 != plane // 2
    second = jnp.where(other, (slot_plane == 0) | (slot_plane == 3), slot_plane != plane)
    number = (2 * other.astype(jnp.int32) + second.astype(jnp.int32)) * owned + slots % owned
    turned = slot_column ^ column
    there = (turned * rest + number - served) * MOST
    here = (COLUMNS * rest + turned * served + number) * MOST
    target = jnp.where(number < served, here, there) + position

    down_own = jnp.swapaxes(slot_down_weight, 1, 2)
    up_own = slot_up_weight
    tp = lax.axis_index("tp")
    tiles = query_weight.shape[1] // 2 // TILE
    first, second = tiles // 4, tiles * 5 // 8
    down_pair = send(down_own, pair)
    down_near = send(down_own, across)

    packed = pack(target[None, :], hidden_input, [rest * MOST] * COLUMNS + [served * MOST] * COLUMNS)
    away, home = packed[:COLUMNS], packed[COLUMNS:]
    away = [away[0]] + [send(away[d], turn[d]) for d in range(1, COLUMNS)]
    given, own = project(tp, after(hidden_input, home[0]), query_weight, [(True, 0, tiles), (False, 0, first)])
    base_own = [own]

    up_pair = send(up_own, pair, down_pair, given)
    up_near = send(up_own, across, down_near, given)
    beside = [home[0]] + [send(home[d], turn[d], away[d], given) for d in (1, 2)]
    moving = join(away)
    base_own += project(tp, after(hidden_input, down_pair, down_near, moving), query_weight, [(False, first, second - first)])

    moved = send(moving, inward, up_pair, base_own[1])
    down_out = send(down_near[:cut], outward, up_pair, base_own[1])
    up_far = send(up_pair, across, up_near, base_own[1])
    beside.append(send(home[3], turn[3], beside[1], beside[2], base_own[1]))
    late = after(hidden_input, beside[1], beside[2], up_near)
    base_own += project(tp, late, query_weight, [(False, second, tiles - second)])
    down_far = send(down_pair, across, up_far, down_out)
    up_near_out = send(up_near, outward, down_out, base_own[2])

    split = COLUMNS * rest * MOST
    spots = lax.broadcasted_iota(jnp.int32, (target.shape[0], 4 * owned * COLUMNS * MOST), 1)
    onehot = (after(target, given)[:, None] == spots).astype(jnp.bfloat16)
    back_away, back_home = onehot[:, :split], onehot[:, split:]

    def swapped(y, *earlier):
        return lax.ppermute(after(y, *earlier) if earlier else y, "tp", SWAP)

    low = down(
        [(after(beside[0], base_own[2]), 0)] + [(rows, 0) for rows in beside[1:]],
        [([down_own], 0, owned), ([down_pair], 0, owned), ([down_near, down_out], 0, cut)],
    )
    up_far_out = send(up_far, outward, up_near_out, low)
    rows = lift(
        [low, swapped(low)], [([up_own], 0, owned), ([up_pair], 0, owned), ([up_near, up_near_out], 0, cut)]
    )
    lifted_home = [rows[0]] + [send(rows[d], turn[d]) for d in (1, 2)]
    lifted_home.append(send(rows[3], turn[3], lifted_home[1]))

    low = down(
        [(after(away[0], up_far_out, lifted_home[1], lifted_home[2]), 0)]
        + [(rows, 0) for rows in away[1:]]
        + [(moved, d) for d in range(COLUMNS)],
        [([down_near], cut, owned - cut), ([down_far], 0, owned)],
    )
    low_other = swapped(low)
    base_other = swapped(given, low_other)
    low = (low + low_other).astype(jnp.bfloat16)
    rows = lift(
        [low, send(low[low.shape[0] // 2 :], outward)],
        [([up_near, up_near_out], cut, owned - cut), ([up_far, up_far_out], 0, owned)],
    )
    lifted_away = [rows[0]] + [send(rows[d], turn[d]) for d in range(1, COLUMNS)]
    base_own[0] = after(base_own[0], rows[0])
    part = finish(back_home, [base_own, [base_other]], lifted_home, TILE, jnp.bfloat16)
    return finish(back_away, [[part]], lifted_away, 2 * TILE, jnp.bfloat16)


def by_gather(hidden_input, query_weight, slot_down_weight, slot_up_weight, request_adapter, adapter_slot):
    local_width = hidden_input.shape[1]
    output_width = slot_up_weight.shape[2]
    total = slot_down_weight.shape[0] * lax.axis_size("rep")
    base_sum = lax.psum_scatter(
        lax.dot_general(
            query_weight, hidden_input, (((0,), (1,)), ((), ())), preferred_element_type=jnp.float32
        ).astype(jnp.bfloat16),
        "tp",
        scatter_dimension=0,
        tiled=True,
    ).astype(jnp.float32)
    slots, position = places(request_adapter, adapter_slot, total)
    target = slots * MOST + position
    buffer = jnp.zeros((total * MOST, local_width), jnp.bfloat16).at[target].set(hidden_input)
    slot_rows = buffer.reshape(total, MOST, local_width)
    lowered = jnp.einsum(
        "amd,adr->amr",
        slot_rows,
        lax.all_gather(slot_down_weight, "rep", axis=0, tiled=True),
        preferred_element_type=jnp.float32,
    )
    lowered = lax.psum(lowered.astype(jnp.bfloat16), "tp")
    lifted = jnp.einsum(
        "amr,are->ame",
        lowered,
        lax.all_gather(slot_up_weight, "rep", axis=0, tiled=True),
        preferred_element_type=jnp.float32,
    )
    lift_rows = lifted.astype(jnp.bfloat16).reshape(total * MOST, output_width)[target]
    return (base_sum.T + lift_rows.astype(jnp.float32)).astype(jnp.bfloat16)


def solution(mesh):
    in_specs = (
        P("rep", "tp"),
        P("tp", None),
        P("rep", "tp", None),
        P("rep", None, "tp"),
        P("rep", None),
        P(),
    )
    out_specs = P("rep", "tp")
    planes = mesh.shape["rep"] == COLUMNS * PLANES and mesh.shape["tp"] == 2
    shards = by_planes if planes else by_gather
    return jax.shard_map(shards, mesh=mesh, in_specs=in_specs, out_specs=out_specs, check_vma=False)
```

```python
import functools

import jax
import jax.numpy as jnp
from jax import lax
from jax.experimental import pallas as pl
from jax.experimental.pallas import tpu as pltpu
from jax.sharding import PartitionSpec as P

MOST = 16
COLUMNS = 4
PLANES = 4
SWAP = [(0, 1), (1, 0)]
LIMIT = 63 * 1024 * 1024
NT = (((1,), (1,)), ((), ()))
TILE = 256


def params(steps=1):
    return pltpu.CompilerParams(dimension_semantics=("arbitrary",) * steps, vmem_limit_bytes=LIMIT)


def cost(flops, size):
    return pl.CostEstimate(flops=flops, bytes_accessed=size, transcendentals=0)


def pack_kernel(target_ref, x_ref, *rest):
    outs, onehot = rest[:-1], rest[-1]

    @pl.when(pl.program_id(0) == 0)
    def _():
        place = lax.broadcasted_iota(jnp.int32, onehot.shape, 0)
        onehot[...] = (place == target_ref[...]).astype(jnp.bfloat16)

    packed = jnp.dot(onehot[...], x_ref[...], preferred_element_type=jnp.float32).astype(jnp.bfloat16)
    at = 0
    for out in outs:
        out[...] = packed[at : at + out.shape[0]]
        at += out.shape[0]


def pack(target, x, parts):
    rows, width = x.shape
    tile = 1024
    return pl.pallas_call(
        pack_kernel,
        grid=(width // tile,),
        in_specs=[pl.BlockSpec((1, rows), lambda i: (0, 0)), pl.BlockSpec((rows, tile), lambda i: (0, i))],
        out_specs=[pl.BlockSpec((part, tile), lambda i: (0, i)) for part in parts],
        out_shape=[jax.ShapeDtypeStruct((part, width), x.dtype) for part in parts],
        scratch_shapes=[pltpu.VMEM((sum(parts), rows), jnp.bfloat16)],
        compiler_params=params(),
        cost_estimate=cost(2 * sum(parts) * rows * width, 2 * (rows + sum(parts)) * width),
        name="pack_rows",
    )(target, x)


def project_kernel(counts, place_ref, x_ref, w_ref, *outs):
    step, at = pl.program_id(0), 0
    product = jnp.dot(x_ref[...], w_ref[...], preferred_element_type=jnp.float32).astype(jnp.bfloat16)
    for out, count in zip(outs, counts):

        @pl.when((step >= at) & (step < at + count))
        def _():
            out[...] = product

        at += count


def project(tp, x, w, parts):
    rows, width = x.shape
    tile = TILE
    steps = w.shape[1] // 2 // tile
    counts = [count for _, _, count in parts]
    firsts = jnp.stack([(1 - tp if given else tp) * steps + first for given, first, _ in parts])
    columns = sum(counts) * tile

    def w_tile(i, place):
        at, found = 0, place[0] + i
        for k, count in enumerate(counts):
            found = jnp.where(i >= at, place[k] + i - at, found)
            at += count
        return 0, found

    def out_spec(at, count):
        return pl.BlockSpec((rows, tile), lambda i, place: (0, jnp.clip(i - at, 0, count - 1)))

    return pl.pallas_call(
        functools.partial(project_kernel, counts),
        grid_spec=pltpu.PrefetchScalarGridSpec(
            num_scalar_prefetch=1,
            grid=(sum(counts),),
            in_specs=[
                pl.BlockSpec((rows, width), lambda i, place: (0, 0)),
                pl.BlockSpec((width, tile), w_tile),
            ],
            out_specs=[out_spec(sum(counts[:k]), count) for k, count in enumerate(counts)],
        ),
        out_shape=[jax.ShapeDtypeStruct((rows, count * tile), jnp.bfloat16) for count in counts],
        compiler_params=params(),
        cost_estimate=cost(2 * rows * width * columns, 2 * (rows * width + columns * width + rows * columns)),
        name="project_half",
    )(firsts, x, w)


def factor_specs(groups, rank, tile):
    specs = []
    for arrays, first, count in groups:
        shape = (count, rank, tile)
        specs += [pl.BlockSpec(shape, lambda k, at=first // count: (at, 0, k))] * len(arrays)
    return specs


def factors(refs, groups):
    at = start = 0
    for held, count in groups:
        total = functools.reduce(jnp.add, [ref[...] for ref in refs[at : at + held]])
        yield start, count, total.reshape(count * total.shape[1], total.shape[2])
        at += held
        start += count


def flat(groups):
    return [array for arrays, _, _ in groups for array in arrays]


def shape_of(groups):
    return [(len(arrays), count) for arrays, _, count in groups]


def owned_by(shape, count):
    owner = lax.broadcasted_iota(jnp.int32, shape, 0) // MOST % count
    return owner == lax.broadcasted_iota(jnp.int32, shape, 1) // (shape[1] // count)


def down_kernel(groups, sources, *refs):
    xs, ws, o_ref, total = refs[:sources], refs[sources:-2], refs[-2], refs[-1]
    step = pl.program_id(0)
    rank = o_ref.shape[1]
    sides = sources // COLUMNS
    side_rows = o_ref.shape[0] // sides

    @pl.when(step == 0)
    def _():
        total[...] = jnp.zeros_like(total)

    for start, count, w in factors(ws, groups):
        rows = jnp.concatenate([x[start * MOST : (start + count) * MOST] for x in xs], axis=0)
        at = start * sources * MOST
        total[at : at + rows.shape[0], : w.shape[0]] += lax.dot_general(
            rows, w, NT, preferred_element_type=jnp.float32
        )

    @pl.when(step == pl.num_programs(0) - 1)
    def _():
        start = 0
        for _, count in groups:
            at, part = start * sources * MOST, COLUMNS * count * MOST
            y = total[at : at + sides * part, : count * rank]
            y = jnp.where(owned_by(y.shape, count), y, 0.0)
            y = functools.reduce(jnp.add, [y[:, k * rank : (k + 1) * rank] for k in range(count)])
            for side in range(sides):
                to = side * side_rows + start * COLUMNS * MOST
                o_ref[to : to + part] = y[side * part : (side + 1) * part]
            start += count


def down(xs, groups):
    served = sum(count for _, _, count in groups)
    _, rank, width = groups[0][0][0].shape
    tile = 512
    rows = len(xs) * served * MOST
    wide = max(count for _, _, count in groups) * rank

    def block(section):
        return pl.BlockSpec((served * MOST, tile), lambda k: (section, k))

    return pl.pallas_call(
        functools.partial(down_kernel, shape_of(groups), len(xs)),
        grid=(width // tile,),
        in_specs=[block(section) for _, section in xs] + factor_specs(groups, rank, tile),
        out_specs=pl.BlockSpec((rows, rank), lambda k: (0, 0)),
        out_shape=jax.ShapeDtypeStruct((rows, rank), jnp.float32),
        scratch_shapes=[pltpu.VMEM((rows, wide), jnp.float32)],
        compiler_params=params(),
        cost_estimate=cost(2 * rows * wide * width, 2 * width * (served * rank + rows)),
        name="down_rows",
    )(*[x for x, _ in xs], *flat(groups))


def lift_kernel(groups, count_y, *refs):
    outs, y = refs[-1 - COLUMNS : -1], refs[-1]
    ys, us = refs[:count_y], refs[count_y : -1 - COLUMNS]

    @pl.when(pl.program_id(0) == 0)
    def _():
        low = functools.reduce(jnp.add, [ref[...] for ref in ys]).astype(jnp.float32)
        at = 0
        for _, count in groups:
            part = COLUMNS * count * MOST
            wide = jnp.concatenate([low[at : at + part]] * count, axis=1)
            wide = jnp.where(owned_by(wide.shape, count), wide, 0.0)
            y[at : at + part, : wide.shape[1]] = wide.astype(jnp.bfloat16)
            at += part

    for start, count, u in factors(us, groups):
        part = count * MOST
        at = start * COLUMNS * MOST
        low = y[at : at + COLUMNS * part, : u.shape[0]]
        rows = jnp.dot(low, u, preferred_element_type=jnp.float32).astype(jnp.bfloat16)
        for k, out in enumerate(outs):
            out[start * MOST : start * MOST + part] = rows[k * part : (k + 1) * part]


def lift(ys, groups):
    served = sum(count for _, _, count in groups)
    _, rank, columns = groups[0][0][0].shape
    tile = 512
    rows, wide = served * COLUMNS * MOST, max(count for _, _, count in groups) * rank
    return pl.pallas_call(
        functools.partial(lift_kernel, shape_of(groups), len(ys)),
        grid=(columns // tile,),
        in_specs=[pl.BlockSpec((rows, rank), lambda k: (0, 0))] * len(ys) + factor_specs(groups, rank, tile),
        out_specs=[pl.BlockSpec((served * MOST, tile), lambda k: (0, k))] * COLUMNS,
        out_shape=[jax.ShapeDtypeStruct((served * MOST, columns), jnp.bfloat16)] * COLUMNS,
        scratch_shapes=[pltpu.VMEM((rows, wide), jnp.bfloat16)],
        compiler_params=params(),
        cost_estimate=cost(2 * rows * wide * columns, 2 * columns * (served * rank + rows)),
        name="lift_rows",
    )(*ys, *flat(groups))


def finish_kernel(starts, onehot_ref, *rest):
    count = sum(len(own) for own in starts)
    bases, pieces, o_ref = rest[:count], rest[count:-1], rest[-1]
    step = pl.program_id(0)
    lifted = jnp.concatenate([piece[...] for piece in pieces], axis=0)
    total = jnp.dot(onehot_ref[...], lifted, preferred_element_type=jnp.float32)
    at = 0
    for own in starts:
        base = bases[at][...]
        for k in range(1, len(own)):
            base = jnp.where(step >= own[k], bases[at + k][...], base)
        total += base.astype(jnp.float32)
        at += len(own)
    o_ref[...] = total.astype(o_ref.dtype)


def finish(onehot, bases, pieces, tile, dtype):
    rows, columns = onehot.shape[0], pieces[0].shape[1]
    held = onehot.shape[1]
    starts, specs = [], []
    for arrays in bases:
        at, own = 0, []
        for array in arrays:
            steps = array.shape[1] // tile
            own.append(at)
            specs.append(pl.BlockSpec((rows, tile), lambda i, at=at, steps=steps: (0, jnp.clip(i - at, 0, steps - 1))))
            at += steps
        starts.append(own)
    return pl.pallas_call(
        functools.partial(finish_kernel, starts),
        grid=(columns // tile,),
        in_specs=[pl.BlockSpec((rows, held), lambda i: (0, 0)), *specs]
        + [pl.BlockSpec((piece.shape[0], tile), lambda i: (0, i)) for piece in pieces],
        out_specs=pl.BlockSpec((rows, tile), lambda i: (0, i)),
        out_shape=jax.ShapeDtypeStruct((rows, columns), dtype),
        compiler_params=params(),
        cost_estimate=cost(2 * rows * held * columns, 8 * rows * columns),
        name="finish_rows",
    )(onehot, *[array for arrays in bases for array in arrays], *pieces)


def join_kernel(*refs):
    pieces, o_ref = refs[:-1], refs[-1]
    rows = pieces[0].shape[0]
    for k, piece in enumerate(pieces):
        o_ref[k * rows : (k + 1) * rows] = piece[...]


def join(pieces):
    rows, width = pieces[0].shape
    tile = 1024
    return pl.pallas_call(
        join_kernel,
        grid=(width // tile,),
        in_specs=[pl.BlockSpec((rows, tile), lambda k: (0, k))] * len(pieces),
        out_specs=pl.BlockSpec((rows * len(pieces), tile), lambda k: (0, k)),
        out_shape=jax.ShapeDtypeStruct((rows * len(pieces), width), pieces[0].dtype),
        compiler_params=params(),
        cost_estimate=cost(0, 4 * rows * len(pieces) * width),
        name="join_rows",
    )(*pieces)


def places(request_adapter, adapter_slot, total):
    rows = request_adapter.shape[0]
    ids = request_adapter[:, 0]
    names = lax.broadcasted_iota(jnp.int32, (rows, total), 1)
    slots = jnp.sum(jnp.where(ids[:, None] == names, adapter_slot[None, :], 0), axis=1)
    onehot = (slots[:, None] == names).astype(jnp.bfloat16)
    row_iota = lax.broadcasted_iota(jnp.int32, (rows, rows), 0)
    col_iota = lax.broadcasted_iota(jnp.int32, (rows, rows), 1)
    earlier = (row_iota > col_iota).astype(jnp.bfloat16)
    counts = jnp.dot(earlier, onehot, preferred_element_type=jnp.float32)
    position = jnp.sum(counts * onehot.astype(jnp.float32), axis=1).astype(jnp.int32)
    return slots, position


def after(x, *earlier):
    return lax.optimization_barrier((x, *earlier))[0]


def by_planes(hidden_input, query_weight, slot_down_weight, slot_up_weight, request_adapter, adapter_slot):
    owned = slot_down_weight.shape[0]
    cut = owned // 2
    served = 2 * owned + cut
    rest = 4 * owned - served
    me = lax.axis_index("rep")
    plane, column = me // COLUMNS, me % COLUMNS
    every = range(COLUMNS * PLANES)
    inside = [r for r in every if r // COLUMNS in (1, 2)]
    outside = [r for r in every if r // COLUMNS in (0, 3)]

    def send(x, pairs, *earlier):
        return lax.ppermute(after(x, *earlier) if earlier else x, "rep", pairs)

    pair = [(r, r ^ 4) for r in every]
    across = [(r, r ^ 12) for r in inside]
    outward = [(r, r ^ 4) for r in inside]
    inward = [(r, r ^ 4) for r in outside]
    turn = [[(r, r ^ d) for r in every] for d in range(COLUMNS)]

    slots, position = places(request_adapter, adapter_slot, owned * COLUMNS * PLANES)
    slot_plane = slots // (owned * COLUMNS)
    slot_column = slots // owned % COLUMNS
    other = slot_plane // 2 != plane // 2
    second = jnp.where(other, (slot_plane == 0) | (slot_plane == 3), slot_plane != plane)
    number = (2 * other.astype(jnp.int32) + second.astype(jnp.int32)) * owned + slots % owned
    turned = slot_column ^ column
    there = (turned * rest + number - served) * MOST
    here = (COLUMNS * rest + turned * served + number) * MOST
    target = jnp.where(number < served, here, there) + position

    down_own = jnp.swapaxes(slot_down_weight, 1, 2)
    up_own = slot_up_weight
    tp = lax.axis_index("tp")
    tiles = query_weight.shape[1] // 2 // TILE
    first, second = tiles // 4, tiles * 5 // 8
    down_pair = send(down_own, pair)
    down_near = send(down_own, across)

    packed = pack(target[None, :], hidden_input, [rest * MOST] * COLUMNS + [served * MOST] * COLUMNS)
    away, home = packed[:COLUMNS], packed[COLUMNS:]
    away = [away[0]] + [send(away[d], turn[d]) for d in range(1, COLUMNS)]
    given, own = project(tp, after(hidden_input, home[0]), query_weight, [(True, 0, tiles), (False, 0, first)])
    base_own = [own]

    up_pair = send(up_own, pair, down_pair, given)
    up_near = send(up_own, across, down_near, given)
    beside = [home[0]] + [send(home[d], turn[d], away[d], given) for d in (1, 2)]
    moving = join(away)
    base_own += project(tp, after(hidden_input, down_pair, down_near, moving), query_weight, [(False, first, second - first)])

    moved = send(moving, inward, up_pair, base_own[1])
    down_out = send(down_near[:cut], outward, up_pair, base_own[1])
    up_far = send(up_pair, across, up_near, base_own[1])
    beside.append(send(home[3], turn[3], beside[1], beside[2], base_own[1]))
    late = after(hidden_input, beside[1], beside[2], up_near)
    base_own += project(tp, late, query_weight, [(False, second, tiles - second)])
    down_far = send(down_pair, across, up_far, down_out)
    up_near_out = send(up_near, outward, down_out, base_own[2])

    split = COLUMNS * rest * MOST
    spots = lax.broadcasted_iota(jnp.int32, (target.shape[0], 4 * owned * COLUMNS * MOST), 1)
    onehot = (after(target, given)[:, None] == spots).astype(jnp.bfloat16)
    back_away, back_home = onehot[:, :split], onehot[:, split:]

    def swapped(y, *earlier):
        return lax.ppermute(after(y, *earlier) if earlier else y, "tp", SWAP)

    low = down(
        [(after(beside[0], base_own[2]), 0)] + [(rows, 0) for rows in beside[1:]],
        [([down_own], 0, owned), ([down_pair], 0, owned), ([down_near, down_out], 0, cut)],
    )
    up_far_out = send(up_far, outward, up_near_out, low)
    rows = lift(
        [low, swapped(low)], [([up_own], 0, owned), ([up_pair], 0, owned), ([up_near, up_near_out], 0, cut)]
    )
    lifted_home = [rows[0]] + [send(rows[d], turn[d]) for d in (1, 2)]
    lifted_home.append(send(rows[3], turn[3], lifted_home[1]))

    low = down(
        [(after(away[0], up_far_out, lifted_home[1], lifted_home[2]), 0)]
        + [(rows, 0) for rows in away[1:]]
        + [(moved, d) for d in range(COLUMNS)],
        [([down_near], cut, owned - cut), ([down_far], 0, owned)],
    )
    low_other = swapped(low)
    base_other = swapped(given, low_other)
    low = (low + low_other).astype(jnp.bfloat16)
    rows = lift(
        [low, send(low[low.shape[0] // 2 :], outward)],
        [([up_near, up_near_out], cut, owned - cut), ([up_far, up_far_out], 0, owned)],
    )
    lifted_away = [rows[0]] + [send(rows[d], turn[d]) for d in range(1, COLUMNS)]
    base_own[0] = after(base_own[0], rows[0])
    part = finish(back_home, [base_own, [base_other]], lifted_home, TILE, jnp.bfloat16)
    return finish(back_away, [[part]], lifted_away, 2 * TILE, jnp.bfloat16)


def by_gather(hidden_input, query_weight, slot_down_weight, slot_up_weight, request_adapter, adapter_slot):
    local_width = hidden_input.shape[1]
    output_width = slot_up_weight.shape[2]
    total = slot_down_weight.shape[0] * lax.axis_size("rep")
    base_sum = lax.psum_scatter(
        lax.dot_general(
            query_weight, hidden_input, (((0,), (1,)), ((), ())), preferred_element_type=jnp.float32
        ).astype(jnp.bfloat16),
        "tp",
        scatter_dimension=0,
        tiled=True,
    ).astype(jnp.float32)
    slots, position = places(request_adapter, adapter_slot, total)
    target = slots * MOST + position
    buffer = jnp.zeros((total * MOST, local_width), jnp.bfloat16).at[target].set(hidden_input)
    slot_rows = buffer.reshape(total, MOST, local_width)
    lowered = jnp.einsum(
        "amd,adr->amr",
        slot_rows,
        lax.all_gather(slot_down_weight, "rep", axis=0, tiled=True),
        preferred_element_type=jnp.float32,
    )
    lowered = lax.psum(lowered.astype(jnp.bfloat16), "tp")
    lifted = jnp.einsum(
        "amr,are->ame",
        lowered,
        lax.all_gather(slot_up_weight, "rep", axis=0, tiled=True),
        preferred_element_type=jnp.float32,
    )
    lift_rows = lifted.astype(jnp.bfloat16).reshape(total * MOST, output_width)[target]
    return (base_sum.T + lift_rows.astype(jnp.float32)).astype(jnp.bfloat16)


def solution(mesh):
    in_specs = (
        P("rep", "tp"),
        P("tp", None),
        P("rep", "tp", None),
        P("rep", None, "tp"),
        P("rep", None),
        P(),
    )
    out_specs = P("rep", "tp")
    planes = mesh.shape["rep"] == COLUMNS * PLANES and mesh.shape["tp"] == 2
    shards = by_planes if planes else by_gather
    return jax.shard_map(shards, mesh=mesh, in_specs=in_specs, out_specs=out_specs, check_vma=False)
```
